32 devices in a mesh: row: 4 (over x, core), col: 8 (over z, y).
Axes of the slice: x: 2, y: 2, z: 4, core: 2. Of those that a mesh axis runs over, the one named last changes fastest.
Arguments:
- features: float32 [4096, 512], P(('col', 'row')), may hold values from -6 to 6
- weight: float32 [512, 512], replicated, may hold values from -0.25 to 0.25
- cotangent: bfloat16 [4096, 512], P(('row', 'col')), may hold values from -6 to 6
- block_values: bfloat16 [4, 8, 12, 128, 128], P('row', 'col'), may hold values from -0.1875 to 0.1875
- block_coords: int32 [4, 8, 2, 12], P('row', 'col'), may hold values from -1 to 7, as said below
Outputs:
- activated: float32 [4096, 512], P(('row', 'col'))
- dfeatures: float32 [4096, 512], P(('col', 'row'))
- dweight: float32 [512, 512], P('row', 'col')
The draws below stay inside these ranges and needn't reach their ends.
Inputs may be any that keep to these rules, and one draw needn't show every extreme that they name: block_coords[r, c, 0, s] is a block row below 8 and block_coords[r, c, 1, s] a block column below 4 of slot s of device (r, c), or both are -1 for an unused slot. Used slots come first and name distinct blocks; each device uses between a quarter of 12 (rounded down) and all 12 slots, and some device uses all 12.
All inputs are finite; a program needn't handle non-finite values.
Results may differ from the reference program's by a relative error of at most 0.006.
Values may be sent and summed in bfloat16 or wider, within the bound.
A program may use at most 128 MiB of HBM per device.

```python
import jax
import jax.numpy as jnp
from jax import lax

HID = 512
BLK = 128
ROWS_DEV = 128
NODES = 4096
RBLOCKS = 8
CBLOCKS = 4
NB = 12
N_ROW = 4
N_COL = 8


def draw_block_coords(key, part):
    base_key = jax.random.fold_in(key, 7)
    key_count, key_full, key_order = jax.random.split(base_key, 3)
    device_total = N_ROW * N_COL
    slot_total = RBLOCKS * CBLOCKS
    live_count = jax.random.randint(key_count, (device_total,), NB // 4, NB + 1)
    full_device = jax.random.randint(key_full, (), 0, device_total)
    live_count = jnp.where(jnp.arange(device_total) == full_device, NB, live_count)
    order_keys = jax.random.split(key_order, device_total)
    chosen = jax.vmap(lambda single: jax.random.permutation(single, slot_total)[:NB])(order_keys)
    live_slots = jnp.arange(NB)[None, :] < live_count[:, None]
    row_ids = jnp.where(live_slots, chosen // CBLOCKS, -1)
    col_ids = jnp.where(live_slots, chosen % CBLOCKS, -1)
    return jnp.stack([row_ids, col_ids], axis=1).reshape(N_ROW, N_COL, 2, NB).astype(jnp.int32)


def block_levels(key, extent, shards, low, top_value):
    level, own = 1.0, jax.random.fold_in(key, 6)
    for dim, blocks in shards:
        heights = jnp.exp(jax.random.uniform(jax.random.fold_in(own, dim), (blocks,), jnp.float32, low / len(shards), top_value / len(shards)))
        level = level * jnp.repeat(heights, extent[dim] // blocks).reshape([-1 if axis == dim else 1 for axis in range(len(extent))])
    return level


def gaussian(rng, dims, spread, reach, shards=(), kind=jnp.bfloat16):
    result = spread * jax.random.normal(rng, dims, jnp.float32)
    if shards:
        result = result * block_levels(rng, dims, shards, -0.22, 0.18)
    return jnp.clip(result, -reach, reach).astype(kind)


def setup_inputs(seed: int = 0) -> dict:
    arg_keys = jax.random.split(jax.random.key(seed), 6)
    features = gaussian(arg_keys[0], (NODES, HID), 1.0, 6.0, ((0, 32),), jnp.float32)
    weight = gaussian(arg_keys[1], (HID, HID), HID ** -0.5, 0.25, (), jnp.float32)
    cotangent = gaussian(arg_keys[2], (NODES, HID), 1.0, 6.0, ((0, 32),))
    block_values = gaussian(arg_keys[3], (N_ROW, N_COL, NB, BLK, BLK), (N_ROW * N_COL * ROWS_DEV // 4) ** -0.5, 0.1875, ((0, 4), (1, 8)))
    block_coords = draw_block_coords(jax.random.fold_in(arg_keys[5], 71), 0)
    return {"features": features, "weight": weight, "cotangent": cotangent, "block_values": block_values, "block_coords": block_coords}


def silu_slope(values):
    sigma = jax.nn.sigmoid(values)
    return sigma * (1.0 + values * (1.0 - sigma))


def forward_tile(slot_values, coordinate, tile_stack):
    slot_rows = coordinate[0]
    slot_cols = coordinate[1]
    live_slots = slot_rows >= 0
    masked = jnp.where(live_slots[:, None, None], slot_values.astype(jnp.float32), jnp.float32(0.0))
    selected = tile_stack[jnp.maximum(slot_cols, 0).astype(jnp.int32)].astype(jnp.float32)
    products = jnp.einsum("sab,sbc->sac", masked, selected)
    return jax.ops.segment_sum(products, jnp.maximum(slot_rows, 0).astype(jnp.int32), num_segments=RBLOCKS)


def backward_tile(slot_values, coordinate, tile_stack):
    slot_rows = coordinate[0]
    slot_cols = coordinate[1]
    live_slots = slot_rows >= 0
    masked = jnp.where(live_slots[:, None, None], slot_values.astype(jnp.float32), jnp.float32(0.0))
    selected = tile_stack[jnp.maximum(slot_rows, 0).astype(jnp.int32)].astype(jnp.float32)
    products = jnp.einsum("sab,sac->sbc", masked, selected)
    return jax.ops.segment_sum(products, jnp.maximum(slot_cols, 0).astype(jnp.int32), num_segments=CBLOCKS)


def reference(features, weight, cotangent, block_values, block_coords):
    xcopy = features.astype(jnp.bfloat16)
    wcopy = weight.astype(jnp.bfloat16)
    projected = jnp.dot(xcopy, wcopy, preferred_element_type=jnp.float32).astype(jnp.bfloat16)
    column_tiles = projected.reshape(N_COL, CBLOCKS, BLK, HID)

    def row_range(row_index):
        def add_device(totals, col_index):
            term = forward_tile(block_values[row_index, col_index], block_coords[row_index, col_index], column_tiles[col_index])
            return totals + term, None

        zero_sums = jnp.zeros((RBLOCKS, BLK, HID), jnp.float32)
        totals, _ = lax.scan(add_device, zero_sums, jnp.arange(N_COL, dtype=jnp.int32))
        return totals

    aggregate = lax.map(row_range, jnp.arange(N_ROW, dtype=jnp.int32)).reshape(NODES, HID)
    activated = jax.nn.silu(aggregate)
    slope = (cotangent.astype(jnp.float32) * silu_slope(aggregate)).astype(jnp.bfloat16)
    row_tiles = slope.reshape(N_ROW, RBLOCKS, BLK, HID)

    def column_range(col_index):
        def add_device(totals, row_index):
            term = backward_tile(block_values[row_index, col_index], block_coords[row_index, col_index], row_tiles[row_index])
            return totals + term, None

        zero_sums = jnp.zeros((CBLOCKS, BLK, HID), jnp.float32)
        totals, _ = lax.scan(add_device, zero_sums, jnp.arange(N_ROW, dtype=jnp.int32))
        return totals

    node_grad = lax.map(column_range, jnp.arange(N_COL, dtype=jnp.int32)).reshape(NODES, HID)
    grad_copy = node_grad.astype(jnp.bfloat16)
    dfeatures = jnp.dot(grad_copy, wcopy.T, preferred_element_type=jnp.float32)
    dweight = jnp.dot(xcopy.T, grad_copy, preferred_element_type=jnp.float32) * (1.0 / NODES ** 0.5)
    return activated, dfeatures, dweight
```

```python
import functools

import jax
import jax.numpy as jnp
from jax import lax
from jax.experimental import pallas as pl
from jax.experimental.pallas import tpu as pltpu
from jax.sharding import PartitionSpec as P

MESH = pl.DeviceIdType.MESH
PARTS = 2
F32, BF16 = jnp.float32, jnp.bfloat16


def each(count, body):
    if count <= 8:
        for k in range(count):
            body(k)
    else:
        lax.fori_loop(0, count, lambda k, carry: (body(k), carry)[1], 0)


def inner_size(count):
    return 2 if count % 2 == 0 else 1


def dot(a, b, left=1, right=0):
    return lax.dot_general(a, b, (((left,), (right,)), ((), ())), preferred_element_type=F32)


def remote(src, dst, sent, landed, device):
    return pltpu.make_async_remote_copy(
        src_ref=src, dst_ref=dst, send_sem=sent, recv_sem=landed, device_id=device, device_id_type=MESH
    )


class Line:
    def __init__(self, name, count, device):
        self.count, self.device = count, device
        self.inner = inner_size(count)
        self.outer = count // self.inner
        self.me = lax.axis_index(name)
        self.o = self.me // self.inner
        self.i = self.me % self.inner

    def ahead(self, k):
        return lax.rem(self.o + k + 1, self.outer)

    def behind(self, k):
        return lax.rem(self.o + self.outer - k - 1, self.outer)

    def mate(self):
        return self.device(self.o * self.inner + 1 - self.i)


class Gather:
    def __init__(self, line, buf, sent, landed):
        self.line, self.buf, self.sent, self.landed = line, buf, sent, landed

    def copy(self, h, index, slot, device):
        piece = self.buf.at[h, index]
        return remote(piece, piece, self.sent.at[h, slot], self.landed.at[h, index], device)

    def start(self, h):
        line = self.line

        def far(k):
            self.copy(h, line.me, k, line.device(line.ahead(k) * line.inner + line.i)).start()

        if line.inner == 2:
            self.copy(h, line.me, line.outer - 1, line.mate()).start()
        each(line.outer - 1, far)

    def any_peer(self):
        line = self.line
        return line.device(lax.rem(line.me + 1, line.count))

    def relay(self, h, k):
        line = self.line
        index = line.behind(k) * line.inner + line.i
        self.copy(h, index, k, self.any_peer()).wait_recv()
        if line.inner == 2:
            self.copy(h, index, line.outer + k, line.mate()).start()
        return index

    def passed(self, h, k):
        line = self.line
        index = line.behind(k - 1) * line.inner + 1 - line.i
        self.copy(h, index, 0, self.any_peer()).wait_recv()
        return index

    def drain(self, h):
        line = self.line
        slots = 2 * line.outer - 1 if line.inner == 2 else line.outer - 1
        each(slots, lambda k: self.copy(h, line.me, k, self.any_peer()).wait_send())


class Scatter:
    def __init__(self, line, near, near_in, far, far_in, total, sems):
        self.line, self.total = line, total
        self.near, self.near_in, self.far, self.far_in = near, near_in, far, far_in
        self.near_sent, self.near_landed, self.far_sent, self.far_landed = sems

    def near_copy(self, h, o2):
        return remote(
            self.near.at[h, o2], self.near_in.at[h, o2], self.near_sent.at[h, o2],
            self.near_landed.at[h, o2], self.line.mate(),
        )

    def far_copy(self, h, o2, source):
        return remote(
            self.far.at[h, o2], self.far_in.at[h, source], self.far_sent.at[h, o2],
            self.far_landed.at[h, source], self.line.device(o2 * self.line.inner + self.line.i),
        )

    def start(self, h, partial):
        line = self.line

        def one(k):
            o2 = line.ahead(k)
            self.near[h, o2] = partial(h, o2 * line.inner + 1 - line.i).astype(BF16)
            self.near_copy(h, o2).start()

        if line.inner == 2:
            each(line.outer, one)

    def pair(self, h, o2, partial):
        line = self.line
        value = partial(h, o2 * line.inner + line.i)
        if line.inner == 2:
            self.near_copy(h, o2).wait_recv()
            value = value + self.near_in[h, o2].astype(F32)
        return value

    def middle(self, h, partial):
        line = self.line

        def one(k):
            o2 = line.ahead(k)
            self.far[h, o2] = self.pair(h, o2, partial).astype(BF16)
            self.far_copy(h, o2, line.o).start()

        each(line.outer - 1, one)
        self.total[h] = self.pair(h, line.o, partial)

    def end(self, h):
        line = self.line

        def one(k):
            source = line.behind(k)
            self.far_copy(h, line.ahead(0), source).wait_recv()
            self.total[h] += self.far_in[h, source].astype(F32)

        each(line.outer - 1, one)
        return self.total[h]

    def drain(self, h):
        line = self.line
        if line.inner == 2:
            each(line.outer, lambda k: self.near_copy(h, k).wait_send())
        each(line.outer - 1, lambda k: self.far_copy(h, line.ahead(k), line.o).wait_send())


def kernel(
    rows_n, cols_n, scale,
    coords, features, weight, cotangent, values,
    activated, dfeatures, dweight,
    xg, xg_sent, xg_landed,
    dense, flipped,
    c_near, c_near_in, c_far, c_far_in, c_total, c_ns, c_nl, c_fs, c_fl,
    sg, sg_sent, sg_landed,
    grad,
    e_near, e_near_in, e_far, e_far_in, e_total, e_ns, e_nl, e_fs, e_fl,
    w1, w1_in, w1_sent, w1_landed,
    w2, w2_in, w2_sent, w2_landed,
    wcopy,
):
    r, c = lax.axis_index("row"), lax.axis_index("col")
    row = Line("row", rows_n, lambda index: (index, c))
    col = Line("col", cols_n, lambda index: (r, index))
    own, hidden = features.shape
    width = hidden // PARTS
    slots, block = values.shape[0], values.shape[1]

    barrier = pltpu.get_barrier_semaphore()
    each(rows_n - 1, lambda k: pl.semaphore_signal(
        barrier, inc=1, device_id=row.device(lax.rem(r + k + 1, rows_n)), device_id_type=MESH))
    each(cols_n - 1, lambda k: pl.semaphore_signal(
        barrier, inc=1, device_id=col.device(lax.rem(c + k + 1, cols_n)), device_id_type=MESH))
    for h in range(PARTS):
        xg[h, r] = features[:, h * width:(h + 1) * width].astype(BF16)
    pl.semaphore_wait(barrier, rows_n + cols_n - 2)

    xs = Gather(row, xg, xg_sent, xg_landed)
    for h in range(PARTS):
        xs.start(h)

    wcopy[...] = weight[...].astype(BF16)
    row_blocks, col_blocks = cols_n * own // block, rows_n * own // block
    per = own // block

    def place(i):
        for j in range(col_blocks):
            def look(s, found):
                same = jnp.logical_and(coords[0, s] == i, coords[1, s] == j)
                return jnp.where(same, s, found)

            found = jnp.int32(slots)
            if slots <= 16:
                for s in range(slots):
                    found = look(s, found)
            else:
                found = lax.fori_loop(0, slots, look, found)
            piece = values[jnp.minimum(found, slots - 1)].astype(F32)
            piece = jnp.where(found < slots, piece, 0.0)
            if per == 1:
                rows, lead = pl.ds(0, block), i
            else:
                rows, lead = pl.ds((i % per) * block, block), i // per
            dense[lead, rows, j * block:(j + 1) * block] = piece.astype(BF16)
            flipped[lead, j * block:(j + 1) * block, rows] = piece.T.astype(BF16)

    each(row_blocks, place)

    agg = Scatter(col, c_near, c_near_in, c_far, c_far_in, c_total, (c_ns, c_nl, c_fs, c_fl))

    def forward(h, index):
        return dot(dense[index], xg[h].reshape(rows_n * own, width))

    for h in range(PARTS):
        each(row.outer - 1, lambda k: xs.relay(h, k))
        if row.inner == 2:
            each(row.outer, lambda k: xs.passed(h, k))
        agg.start(h, forward)
    for h in range(PARTS):
        agg.middle(h, forward)
    mixed = jnp.concatenate([agg.end(h) for h in range(PARTS)], axis=1)
    mixed16 = mixed.astype(BF16)

    slopes = Gather(col, sg, sg_sent, sg_landed)
    for h in range(PARTS):
        span = slice(h * width, (h + 1) * width)
        total = dot(mixed16, wcopy[:, span])
        sigma = jax.nn.sigmoid(total)
        slope = cotangent[:, span].astype(F32) * (sigma * (1.0 + total * (1.0 - sigma)))
        sg[h, c] = slope.astype(BF16)
        slopes.start(h)
        activated[:, span] = total * sigma

    share = hidden // rows_n
    for h in range(PARTS):
        span = slice(h * width, (h + 1) * width)
        w1[:, :, span] = dot(mixed16, sg[h, c], 0, 0).reshape(rows_n, share, width).astype(BF16)

    def w1_copy(k):
        to = lax.rem(r + k + 1, rows_n)
        return remote(w1.at[to], w1_in.at[r], w1_sent.at[to], w1_landed.at[r], row.device(to))

    each(rows_n - 1, lambda k: w1_copy(k).start())

    def backward(h, index):
        return dot(flipped[index], sg[h, index])

    def add(h, index):
        grad[h] += backward(h, index)

    for h in range(PARTS):
        grad[h] = backward(h, c)
        each(col.outer - 1, lambda k: add(h, slopes.relay(h, k)))

    nodes = Scatter(row, e_near, e_near_in, e_far, e_far_in, e_total, (e_ns, e_nl, e_fs, e_fl))

    def term(h, index):
        return grad[h, pl.ds(pl.multiple_of(index * own, own), own), :]

    def w1_wait(k):
        source = lax.rem(r + rows_n - k - 1, rows_n)
        remote(w1.at[source], w1_in.at[source], w1_sent.at[source], w1_landed.at[source],
               row.device(source)).wait_recv()
        return source

    def w2_copy(k):
        to = lax.rem(c + k + 1, cols_n)
        return remote(w2.at[to], w2_in.at[c], w2_sent.at[to], w2_landed.at[c], col.device(to))

    def w2_wait(k):
        source = lax.rem(c + cols_n - k - 1, cols_n)
        remote(w2.at[source], w2_in.at[source], w2_sent.at[source], w2_landed.at[source],
               col.device(source)).wait_recv()

    for h in range(PARTS):
        if col.inner == 2:
            each(col.outer, lambda k: add(h, slopes.passed(h, k)))
        nodes.start(h, term)
        if h == 0:
            each(rows_n - 1, w1_wait)
            w1_in[r] = w1[r]
            weight_sum = jnp.sum(w1_in[...].astype(F32), axis=0)
            w2[...] = weight_sum.T.reshape(cols_n, hidden // cols_n, share).astype(w2.dtype)
            each(cols_n - 1, lambda k: w2_copy(k).start())
            w2_in[c] = w2[c]
        nodes.middle(h, term)

    out = None
    for h in range(PARTS):
        grad16 = nodes.end(h).astype(BF16)
        piece = dot(grad16, wcopy[:, h * width:(h + 1) * width], 1, 1)
        out = piece if out is None else out + piece
    dfeatures[...] = out

    each(cols_n - 1, w2_wait)
    dweight[...] = jnp.sum(w2_in[...].astype(F32), axis=0).T * scale

    for h in range(PARTS):
        xs.drain(h)
        agg.drain(h)
        slopes.drain(h)
        nodes.drain(h)
    each(rows_n - 1, lambda k: w1_copy(k).wait_send())
    each(cols_n - 1, lambda k: w2_copy(k).wait_send())


def on_device(rows_n, cols_n, features, weight, cotangent, block_values, block_coords):
    values, coords = block_values[0, 0], block_coords[0, 0]
    own, hidden = features.shape
    width = hidden // PARTS
    row_in, col_in = inner_size(rows_n), inner_size(cols_n)
    row_out, col_out = rows_n // row_in, cols_n // col_in
    scale = 1.0 / (own * rows_n * cols_n) ** 0.5
    share_r, share_c = hidden // rows_n, hidden // cols_n
    dma = pltpu.SemaphoreType.DMA

    def gather_scratch(count, outer):
        return [
            pltpu.VMEM((PARTS, count, own, width), BF16),
            dma((PARTS, 2 * outer)),
            dma((PARTS, count)),
        ]

    def scatter_scratch(outer):
        piece = pltpu.VMEM((PARTS, outer, own, width), BF16)
        return [piece] * 4 + [pltpu.VMEM((PARTS, own, width), F32)] + [dma((PARTS, outer))] * 4

    scratch = (
        gather_scratch(rows_n, row_out)
        + [
            pltpu.VMEM((cols_n, own, rows_n * own), BF16),
            pltpu.VMEM((cols_n, rows_n * own, own), BF16),
        ]
        + scatter_scratch(col_out)
        + gather_scratch(cols_n, col_out)
        + [pltpu.VMEM((PARTS, rows_n * own, width), F32)]
        + scatter_scratch(row_out)
        + [pltpu.VMEM((rows_n, share_r, hidden), BF16)] * 2
        + [dma((rows_n,))] * 2
        + [pltpu.VMEM((cols_n, share_c, share_r), BF16)] * 2
        + [dma((cols_n,))] * 2
        + [pltpu.VMEM((hidden, hidden), BF16)]
    )
    vmem = pl.BlockSpec(memory_space=pltpu.VMEM)
    return pl.pallas_call(
        functools.partial(kernel, rows_n, cols_n, scale),
        out_shape=(
            jax.ShapeDtypeStruct((own, hidden), F32),
            jax.ShapeDtypeStruct((own, hidden), F32),
            jax.ShapeDtypeStruct((share_r, share_c), F32),
        ),
        in_specs=[pl.BlockSpec(memory_space=pltpu.SMEM)] + [vmem] * 4,
        out_specs=(vmem, vmem, vmem),
        scratch_shapes=scratch,
        compiler_params=pltpu.CompilerParams(
            collective_id=0, has_side_effects=True, vmem_limit_bytes=56 * 1024 * 1024
        ),
    )(coords, features, weight, cotangent, values)


def solution(mesh):
    placed = (
        P(("col", "row"), None),
        P(),
        P(("row", "col"), None),
        P("row", "col", None, None, None),
        P("row", "col", None, None),
    )
    return jax.shard_map(
        functools.partial(on_device, mesh.shape["row"], mesh.shape["col"]),
        mesh=mesh,
        in_specs=placed,
        out_specs=(P(("row", "col"), None), P(("col", "row"), None), P("row", "col")),
        check_vma=False,
    )
```

```python
import functools

import jax
import jax.numpy as jnp
from jax import lax
from jax.experimental import pallas as pl
from jax.experimental.pallas import tpu as pltpu
from jax.sharding import PartitionSpec as P

MESH = pl.DeviceIdType.MESH
PARTS = 2
F32, BF16 = jnp.float32, jnp.bfloat16


def each(count, body):
    if count <= 8:
        for k in range(count):
            body(k)
    else:
        lax.fori_loop(0, count, lambda k, carry: (body(k), carry)[1], 0)


def inner_size(count):
    return 2 if count % 2 == 0 else 1


def dot(a, b, left=1, right=0):
    return lax.dot_general(a, b, (((left,), (right,)), ((), ())), preferred_element_type=F32)


def remote(src, dst, sent, landed, device):
    return pltpu.make_async_remote_copy(
        src_ref=src, dst_ref=dst, send_sem=sent, recv_sem=landed, device_id=device, device_id_type=MESH
    )


class Line:
    def __init__(self, name, count, device):
        self.count, self.device = count, device
        self.inner = inner_size(count)
        self.outer = count // self.inner
        self.me = lax.axis_index(name)
        self.o = self.me // self.inner
        self.i = self.me % self.inner

    def ahead(self, k):
        return lax.rem(self.o + k + 1, self.outer)

    def behind(self, k):
        return lax.rem(self.o + self.outer - k - 1, self.outer)

    def mate(self):
        return self.device(self.o * self.inner + 1 - self.i)


class Gather:
    def __init__(self, line, buf, sent, landed):
        self.line, self.buf, self.sent, self.landed = line, buf, sent, landed

    def copy(self, h, index, slot, device):
        piece = self.buf.at[h, index]
        return remote(piece, piece, self.sent.at[h, slot], self.landed.at[h, index], device)

    def start(self, h):
        line = self.line

        def far(k):
            self.copy(h, line.me, k, line.device(line.ahead(k) * line.inner + line.i)).start()

        if line.inner == 2:
            self.copy(h, line.me, line.outer - 1, line.mate()).start()
        each(line.outer - 1, far)

    def any_peer(self):
        line = self.line
        return line.device(lax.rem(line.me + 1, line.count))

    def relay(self, h, k):
        line = self.line
        index = line.behind(k) * line.inner + line.i
        self.copy(h, index, k, self.any_peer()).wait_recv()
        if line.inner == 2:
            self.copy(h, index, line.outer + k, line.mate()).start()
        return index

    def passed(self, h, k):
        line = self.line
        index = line.behind(k - 1) * line.inner + 1 - line.i
        self.copy(h, index, 0, self.any_peer()).wait_recv()
        return index

    def drain(self, h):
        line = self.line
        slots = 2 * line.outer - 1 if line.inner == 2 else line.outer - 1
        each(slots, lambda k: self.copy(h, line.me, k, self.any_peer()).wait_send())


class Scatter:
    def __init__(self, line, near, near_in, far, far_in, total, sems):
        self.line, self.total = line, total
        self.near, self.near_in, self.far, self.far_in = near, near_in, far, far_in
        self.near_sent, self.near_landed, self.far_sent, self.far_landed = sems

    def near_copy(self, h, o2):
        return remote(
            self.near.at[h, o2], self.near_in.at[h, o2], self.near_sent.at[h, o2],
            self.near_landed.at[h, o2], self.line.mate(),
        )

    def far_copy(self, h, o2, source):
        return remote(
            self.far.at[h, o2], self.far_in.at[h, source], self.far_sent.at[h, o2],
            self.far_landed.at[h, source], self.line.device(o2 * self.line.inner + self.line.i),
        )

    def start(self, h, partial):
        line = self.line

        def one(k):
            o2 = line.ahead(k)
            self.near[h, o2] = partial(h, o2 * line.inner + 1 - line.i).astype(BF16)
            self.near_copy(h, o2).start()

        if line.inner == 2:
            each(line.outer, one)

    def pair(self, h, o2, partial):
        line = self.line
        value = partial(h, o2 * line.inner + line.i)
        if line.inner == 2:
            self.near_copy(h, o2).wait_recv()
            value = value + self.near_in[h, o2].astype(F32)
        return value

    def middle(self, h, partial):
        line = self.line

        def one(k):
            o2 = line.ahead(k)
            self.far[h, o2] = self.pair(h, o2, partial).astype(BF16)
            self.far_copy(h, o2, line.o).start()

        each(line.outer - 1, one)
        self.total[h] = self.pair(h, line.o, partial)

    def end(self, h):
        line = self.line

        def one(k):
            source = line.behind(k)
            self.far_copy(h, line.ahead(0), source).wait_recv()
            self.total[h] += self.far_in[h, source].astype(F32)

        each(line.outer - 1, one)
        return self.total[h]

    def drain(self, h):
        line = self.line
        if line.inner == 2:
            each(line.outer, lambda k: self.near_copy(h, k).wait_send())
        each(line.outer - 1, lambda k: self.far_copy(h, line.ahead(k), line.o).wait_send())


def kernel(
    rows_n, cols_n, scale,
    coords, features, weight, cotangent, values,
    activated, dfeatures, dweight,
    xg, xg_sent, xg_landed,
    dense, flipped,
    c_near, c_near_in, c_far, c_far_in, c_total, c_ns, c_nl, c_fs, c_fl,
    sg, sg_sent, sg_landed,
    grad,
    e_near, e_near_in, e_far, e_far_in, e_total, e_ns, e_nl, e_fs, e_fl,
    w1, w1_in, w1_sent, w1_landed,
    w2, w2_in, w2_sent, w2_landed,
    wcopy, wide, mixed, stock, fetched,
):
    r, c = lax.axis_index("row"), lax.axis_index("col")
    row = Line("row", rows_n, lambda index: (index, c))
    col = Line("col", cols_n, lambda index: (r, index))
    own, hidden = features.shape
    width = hidden // PARTS
    slots, block = values.shape[0], values.shape[1]

    barrier = pltpu.get_barrier_semaphore()
    each(rows_n - 1, lambda k: pl.semaphore_signal(
        barrier, inc=1, device_id=row.device(lax.rem(r + k + 1, rows_n)), device_id_type=MESH))
    each(cols_n - 1, lambda k: pl.semaphore_signal(
        barrier, inc=1, device_id=col.device(lax.rem(c + k + 1, cols_n)), device_id_type=MESH))
    fetch_values = pltpu.make_async_copy(values, stock.at[pl.ds(0, slots)], fetched.at[0])
    fetch_weight = pltpu.make_async_copy(weight, wide, fetched.at[1])
    fetch_values.start()
    fetch_weight.start()
    for h in range(PARTS):
        xg[h, r] = features[:, h * width:(h + 1) * width].astype(BF16)
    stock[slots] = jnp.zeros((block, block), BF16)
    pl.semaphore_wait(barrier, rows_n + cols_n - 2)

    xs = Gather(row, xg, xg_sent, xg_landed)
    for h in range(PARTS):
        xs.start(h)

    row_blocks, col_blocks = cols_n * own // block, rows_n * own // block
    per = own // block
    short = slots <= 16
    keys = [coords[0, s] * col_blocks + coords[1, s] for s in range(slots)] if short else None

    def place(i):
        for j in range(col_blocks):
            def look(s, found):
                key = keys[s] if short else coords[0, s] * col_blocks + coords[1, s]
                return jnp.where(key == i * col_blocks + j, s, found)

            found = jnp.int32(slots)
            if short:
                for s in range(slots):
                    found = look(s, found)
            else:
                found = lax.fori_loop(0, slots, look, found)
            piece = stock[found]
            if per == 1:
                rows, lead = pl.ds(0, block), i
            else:
                rows, lead = pl.ds((i % per) * block, block), i // per
            dense[lead, rows, j * block:(j + 1) * block] = piece
            flipped[lead, j * block:(j + 1) * block, rows] = piece.T

    fetch_values.wait()
    half = row_blocks // 2
    each(half, place)
    each(row.outer - 1, lambda k: xs.relay(0, k))
    each(row_blocks - half, lambda k: place(half + k))
    for h in range(1, PARTS):
        each(row.outer - 1, lambda k: xs.relay(h, k))

    agg = Scatter(col, c_near, c_near_in, c_far, c_far_in, c_total, (c_ns, c_nl, c_fs, c_fl))

    def forward(h, index):
        return dot(dense[index], xg[h].reshape(rows_n * own, width))

    for h in range(PARTS):
        if row.inner == 2:
            each(row.outer, lambda k: xs.passed(h, k))
        agg.start(h, forward)
    fetch_weight.wait()
    wcopy[...] = wide[...].astype(BF16)
    for h in range(PARTS):
        agg.middle(h, forward)
    for h in range(PARTS):
        span = slice(h * width, (h + 1) * width)
        part = agg.end(h).astype(BF16)
        mixed[:, span] = part
        term = dot(part, wcopy[span, :])
        activated[...] = term if h == 0 else activated[...] + term
    mixed16 = mixed[...]

    slopes = Gather(col, sg, sg_sent, sg_landed)
    for h in range(PARTS):
        span = slice(h * width, (h + 1) * width)
        total = activated[:, span]
        sigma = jax.nn.sigmoid(total)
        slope = cotangent[:, span].astype(F32) * (sigma * (1.0 + total * (1.0 - sigma)))
        sg[h, c] = slope.astype(BF16)
        slopes.start(h)
        activated[:, span] = total * sigma

    share = hidden // rows_n
    for h in range(PARTS):
        span = slice(h * width, (h + 1) * width)
        w1[:, :, span] = dot(mixed16, sg[h, c], 0, 0).reshape(rows_n, share, width).astype(BF16)

    def w1_copy(k):
        to = lax.rem(r + k + 1, rows_n)
        return remote(w1.at[to], w1_in.at[r], w1_sent.at[to], w1_landed.at[r], row.device(to))

    each(rows_n - 1, lambda k: w1_copy(k).start())

    def backward(h, index):
        return dot(flipped[index], sg[h, index])

    def add(h, index):
        grad[h] += backward(h, index)

    for h in range(PARTS):
        grad[h] = backward(h, c)
        each(col.outer - 1, lambda k: add(h, slopes.relay(h, k)))

    nodes = Scatter(row, e_near, e_near_in, e_far, e_far_in, e_total, (e_ns, e_nl, e_fs, e_fl))

    def term(h, index):
        return grad[h, pl.ds(pl.multiple_of(index * own, own), own), :]

    def w1_wait(k):
        source = lax.rem(r + rows_n - k - 1, rows_n)
        remote(w1.at[source], w1_in.at[source], w1_sent.at[source], w1_landed.at[source],
               row.device(source)).wait_recv()
        return source

    def w2_copy(k):
        to = lax.rem(c + k + 1, cols_n)
        return remote(w2.at[to], w2_in.at[c], w2_sent.at[to], w2_landed.at[c], col.device(to))

    def w2_wait(k):
        source = lax.rem(c + cols_n - k - 1, cols_n)
        remote(w2.at[source], w2_in.at[source], w2_sent.at[source], w2_landed.at[source],
               col.device(source)).wait_recv()

    for h in range(PARTS):
        if col.inner == 2:
            each(col.outer, lambda k: add(h, slopes.passed(h, k)))
        nodes.start(h, term)
        if h == 0:
            each(rows_n - 1, w1_wait)
            w1_in[r] = w1[r]
            weight_sum = jnp.sum(w1_in[...].astype(F32), axis=0)
            w2[...] = weight_sum.T.reshape(cols_n, hidden // cols_n, share).astype(w2.dtype)
            each(cols_n - 1, lambda k: w2_copy(k).start())
            w2_in[c] = w2[c]
        nodes.middle(h, term)

    out = None
    for h in range(PARTS):
        grad16 = nodes.end(h).astype(BF16)
        piece = dot(grad16, wcopy[:, h * width:(h + 1) * width], 1, 1)
        out = piece if out is None else out + piece
    dfeatures[...] = out

    each(cols_n - 1, w2_wait)
    dweight[...] = jnp.sum(w2_in[...].astype(F32), axis=0) * scale

    for h in range(PARTS):
        xs.drain(h)
        agg.drain(h)
        slopes.drain(h)
        nodes.drain(h)
    each(rows_n - 1, lambda k: w1_copy(k).wait_send())
    each(cols_n - 1, lambda k: w2_copy(k).wait_send())


def hand_over(a, b, c, a_out, b_out, c_out, sems):
    copies = [
        pltpu.make_async_copy(src, dst, sems.at[k])
        for k, (src, dst) in enumerate(((a, a_out), (b, b_out), (c, c_out)))
    ]
    for copy in copies:
        copy.start()
    for copy in copies:
        copy.wait()


def on_device(rows_n, cols_n, features, weight, cotangent, block_values, block_coords):
    values, coords = block_values[0, 0], block_coords[0, 0]
    own, hidden = features.shape
    width = hidden // PARTS
    row_in, col_in = inner_size(rows_n), inner_size(cols_n)
    row_out, col_out = rows_n // row_in, cols_n // col_in
    scale = 1.0 / (own * rows_n * cols_n) ** 0.5
    share_r, share_c = hidden // rows_n, hidden // cols_n
    dma = pltpu.SemaphoreType.DMA

    def gather_scratch(count, outer):
        return [
            pltpu.VMEM((PARTS, count, own, width), BF16),
            dma((PARTS, 2 * outer)),
            dma((PARTS, count)),
        ]

    def scatter_scratch(outer):
        piece = pltpu.VMEM((PARTS, outer, own, width), BF16)
        return [piece] * 4 + [pltpu.VMEM((PARTS, own, width), F32)] + [dma((PARTS, outer))] * 4

    scratch = (
        gather_scratch(rows_n, row_out)
        + [
            pltpu.VMEM((cols_n, own, rows_n * own), BF16),
            pltpu.VMEM((cols_n, rows_n * own, own), BF16),
        ]
        + scatter_scratch(col_out)
        + gather_scratch(cols_n, col_out)
        + [pltpu.VMEM((PARTS, rows_n * own, width), F32)]
        + scatter_scratch(row_out)
        + [pltpu.VMEM((rows_n, share_r, hidden), BF16)] * 2
        + [dma((rows_n,))] * 2
        + [pltpu.VMEM((cols_n, share_c, share_r), BF16)] * 2
        + [dma((cols_n,))] * 2
        + [
            pltpu.VMEM((hidden, hidden), BF16),
            pltpu.VMEM((hidden, hidden), F32),
            pltpu.VMEM((own, hidden), BF16),
            pltpu.VMEM((values.shape[0] + 1,) + values.shape[1:], BF16),
            dma((2,)),
        ]
    )
    vmem = pl.BlockSpec(memory_space=pltpu.VMEM)
    anywhere = pl.BlockSpec(memory_space=pl.ANY)
    results = pl.pallas_call(
        functools.partial(kernel, rows_n, cols_n, scale),
        out_shape=(
            jax.ShapeDtypeStruct((own, hidden), F32),
            jax.ShapeDtypeStruct((own, hidden), F32),
            jax.ShapeDtypeStruct((share_c, share_r), F32),
        ),
        in_specs=[pl.BlockSpec(memory_space=pltpu.SMEM), vmem, anywhere, vmem, anywhere],
        out_specs=(vmem, vmem, vmem),
        scratch_shapes=scratch,
        compiler_params=pltpu.CompilerParams(
            collective_id=0, has_side_effects=True, vmem_limit_bytes=56 * 1024 * 1024
        ),
    )(coords, features, weight, cotangent, values)
    ours, theirs, turned = pl.pallas_call(
        hand_over,
        out_shape=tuple(jax.ShapeDtypeStruct(a.shape, a.dtype) for a in results),
        in_specs=[pl.BlockSpec(memory_space=pltpu.HBM)] * 3,
        out_specs=(pl.BlockSpec(memory_space=pltpu.HBM),) * 3,
        scratch_shapes=[dma((3,))],
        compiler_params=pltpu.CompilerParams(vmem_limit_bytes=60 * 1024 * 1024),
    )(*results)
    return ours, theirs, turned.T


def solution(mesh):
    placed = (
        P(("col", "row"), None),
        P(),
        P(("row", "col"), None),
        P("row", "col", None, None, None),
        P("row", "col", None, None),
    )
    return jax.shard_map(
        functools.partial(on_device, mesh.shape["row"], mesh.shape["col"]),
        mesh=mesh,
        in_specs=placed,
        out_specs=(P(("row", "col"), None), P(("col", "row"), None), P("row", "col")),
        check_vma=False,
    )
```

```python
import functools

import jax
import jax.numpy as jnp
from jax import lax
from jax.experimental import pallas as pl
from jax.experimental.pallas import tpu as pltpu
from jax.sharding import PartitionSpec as P

MESH = pl.DeviceIdType.MESH
PARTS = 2
F32, BF16 = jnp.float32, jnp.bfloat16


def each(count, body):
    if count <= 8:
        for k in range(count):
            body(k)
    else:
        lax.fori_loop(0, count, lambda k, carry: (body(k), carry)[1], 0)


def inner_size(count):
    return 2 if count % 2 == 0 else 1


def dot(a, b, left=1, right=0):
    return lax.dot_general(a, b, (((left,), (right,)), ((), ())), preferred_element_type=F32)


def remote(src, dst, sent, landed, device):
    return pltpu.make_async_remote_copy(
        src_ref=src, dst_ref=dst, send_sem=sent, recv_sem=landed, device_id=device, device_id_type=MESH
    )


class Line:
    def __init__(self, name, count, device):
        self.count, self.device = count, device
        self.inner = inner_size(count)
        self.outer = count // self.inner
        self.me = lax.axis_index(name)
        self.o = self.me // self.inner
        self.i = self.me % self.inner

    def ahead(self, k):
        return lax.rem(self.o + k + 1, self.outer)

    def behind(self, k):
        return lax.rem(self.o + self.outer - k - 1, self.outer)

    def mate(self):
        return self.device(self.o * self.inner + 1 - self.i)


class Gather:
    def __init__(self, line, buf, sent, landed):
        self.line, self.buf, self.sent, self.landed = line, buf, sent, landed

    def copy(self, h, index, slot, device):
        piece = self.buf.at[h, index]
        return remote(piece, piece, self.sent.at[h, slot], self.landed.at[h, index], device)

    def start(self, h):
        line = self.line

        def far(k):
            self.copy(h, line.me, k, line.device(line.ahead(k) * line.inner + line.i)).start()

        if line.inner == 2:
            self.copy(h, line.me, line.outer - 1, line.mate()).start()
        each(line.outer - 1, far)

    def any_peer(self):
        line = self.line
        return line.device(lax.rem(line.me + 1, line.count))

    def relay(self, h, k):
        line = self.line
        index = line.behind(k) * line.inner + line.i
        self.copy(h, index, k, self.any_peer()).wait_recv()
        if line.inner == 2:
            self.copy(h, index, line.outer + k, line.mate()).start()
        return index

    def passed(self, h, k):
        line = self.line
        index = line.behind(k - 1) * line.inner + 1 - line.i
        self.copy(h, index, 0, self.any_peer()).wait_recv()
        return index

    def drain(self, h):
        line = self.line
        slots = 2 * line.outer - 1 if line.inner == 2 else line.outer - 1
        each(slots, lambda k: self.copy(h, line.me, k, self.any_peer()).wait_send())


class Chain:
    def __init__(self, line, buf, sent, landed):
        self.line, self.buf, self.sent, self.landed = line, buf, sent, landed

    def copy(self, h, index, way, device):
        piece = self.buf.at[h, index]
        return remote(
            piece, piece, self.sent.at[h, index // self.line.inner, way], self.landed.at[h, index], device
        )

    def side(self, way):
        line = self.line
        step = 1 if way == 0 else -1
        there = line.o + step
        inside = there < line.outer if way == 0 else there >= 0
        device = line.device(lax.rem(there + line.outer, line.outer) * line.inner + line.i)
        return inside, device

    def spread(self, h, index, ways):
        for way in ways:
            inside, device = self.side(way)

            @pl.when(inside)
            def _():
                self.copy(h, index, way, device).start()

        if self.line.inner == 2:
            self.copy(h, index, 2, self.line.mate()).start()

    def start(self, h):
        self.spread(h, self.line.me, (0, 1))

    def other(self):
        line = self.line
        return line.device(lax.rem(line.me + 1, line.count))

    def each_source(self, k, body):
        line = self.line
        for way, source in ((0, line.o - 1 - k), (1, line.o + 1 + k)):
            pl.when(jnp.logical_and(source >= 0, source < line.outer))(
                functools.partial(body, way, source))

    def relay(self, k, hidden_parts, use):
        def arrived(way, source):
            index = source * self.line.inner + self.line.i
            for h in hidden_parts:
                self.copy(h, index, way, self.other()).wait_recv()
                self.spread(h, index, (way,))
            for h in hidden_parts:
                use(h, index)

        self.each_source(k, arrived)

    def passed(self, k, h, use):
        def arrived(way, source):
            index = source * self.line.inner + 1 - self.line.i
            self.copy(h, index, 2, self.other()).wait_recv()
            use(h, index)

        if isinstance(k, int) and k < 0:
            arrived(2, self.line.o)
        else:
            self.each_source(k, arrived)

    def drain(self, h):
        line = self.line

        def one(source):
            index = source * line.inner + line.i
            for way in (0, 1):
                inside, device = self.side(way)
                went = source <= line.o if way == 0 else source >= line.o

                @pl.when(jnp.logical_and(inside, went))
                def _():
                    self.copy(h, index, way, device).wait_send()

            if line.inner == 2:
                self.copy(h, index, 2, line.mate()).wait_send()

        each(line.outer, one)


class Scatter:
    def __init__(self, line, near, near_in, far, far_in, total, sems):
        self.line, self.total = line, total
        self.near, self.near_in, self.far, self.far_in = near, near_in, far, far_in
        self.near_sent, self.near_landed, self.far_sent, self.far_landed = sems

    def near_copy(self, h, o2):
        return remote(
            self.near.at[h, o2], self.near_in.at[h, o2], self.near_sent.at[h, o2],
            self.near_landed.at[h, o2], self.line.mate(),
        )

    def far_copy(self, h, o2, source):
        return remote(
            self.far.at[h, o2], self.far_in.at[h, source], self.far_sent.at[h, o2],
            self.far_landed.at[h, source], self.line.device(o2 * self.line.inner + self.line.i),
        )

    def start(self, h, partial):
        line = self.line

        def one(k):
            o2 = line.ahead(k)
            self.near[h, o2] = partial(h, o2 * line.inner + 1 - line.i).astype(BF16)
            self.near_copy(h, o2).start()

        if line.inner == 2:
            each(line.outer, one)

    def pair(self, h, o2, partial):
        line = self.line
        value = partial(h, o2 * line.inner + line.i)
        if line.inner == 2:
            self.near_copy(h, o2).wait_recv()
            value = value + self.near_in[h, o2].astype(F32)
        return value

    def middle(self, h, partial):
        line = self.line

        def one(k):
            o2 = line.ahead(k)
            self.far[h, o2] = self.pair(h, o2, partial).astype(BF16)
            self.far_copy(h, o2, line.o).start()

        each(line.outer - 1, one)
        self.total[h] = self.pair(h, line.o, partial)

    def end(self, h):
        line = self.line

        def one(k):
            source = line.behind(k)
            self.far_copy(h, line.ahead(0), source).wait_recv()
            self.total[h] += self.far_in[h, source].astype(F32)

        each(line.outer - 1, one)
        return self.total[h]

    def drain(self, h):
        line = self.line
        if line.inner == 2:
            each(line.outer, lambda k: self.near_copy(h, k).wait_send())
        each(line.outer - 1, lambda k: self.far_copy(h, line.ahead(k), line.o).wait_send())


def kernel(
    rows_n, cols_n, scale,
    coords, features, weight, cotangent, values,
    activated, dfeatures, dweight,
    xg, xg_sent, xg_landed,
    dense, flipped,
    c_near, c_near_in, c_far, c_far_in, c_total, c_ns, c_nl, c_fs, c_fl,
    sg, sg_sent, sg_landed,
    grad,
    e_near, e_near_in, e_far, e_far_in, e_total, e_ns, e_nl, e_fs, e_fl,
    w1, w1_in, w1_sent, w1_landed,
    w2, w2_in, w2_sent, w2_landed,
    wcopy, wide, mixed, stock, fetched,
):
    r, c = lax.axis_index("row"), lax.axis_index("col")
    row = Line("row", rows_n, lambda index: (index, c))
    col = Line("col", cols_n, lambda index: (r, index))
    own, hidden = features.shape
    width = hidden // PARTS
    slots, block = values.shape[0], values.shape[1]

    barrier = pltpu.get_barrier_semaphore()
    each(rows_n - 1, lambda k: pl.semaphore_signal(
        barrier, inc=1, device_id=row.device(lax.rem(r + k + 1, rows_n)), device_id_type=MESH))
    each(cols_n - 1, lambda k: pl.semaphore_signal(
        barrier, inc=1, device_id=col.device(lax.rem(c + k + 1, cols_n)), device_id_type=MESH))
    fetch_values = pltpu.make_async_copy(values, stock.at[pl.ds(0, slots)], fetched.at[0])
    fetch_weight = pltpu.make_async_copy(weight, wide, fetched.at[1])
    fetch_values.start()
    fetch_weight.start()
    for h in range(PARTS):
        xg[h, r] = features[:, h * width:(h + 1) * width].astype(BF16)
    stock[slots] = jnp.zeros((block, block), BF16)
    pl.semaphore_wait(barrier, rows_n + cols_n - 2)

    xs = Gather(row, xg, xg_sent, xg_landed)
    for h in range(PARTS):
        xs.start(h)

    row_blocks, col_blocks = cols_n * own // block, rows_n * own // block
    per = own // block
    short = slots <= 16
    keys = [coords[0, s] * col_blocks + coords[1, s] for s in range(slots)] if short else None

    def place(i):
        for j in range(col_blocks):
            def look(s, found):
                key = keys[s] if short else coords[0, s] * col_blocks + coords[1, s]
                return jnp.where(key == i * col_blocks + j, s, found)

            found = jnp.int32(slots)
            if short:
                for s in range(slots):
                    found = look(s, found)
            else:
                found = lax.fori_loop(0, slots, look, found)
            piece = stock[found]
            if per == 1:
                rows, lead = pl.ds(0, block), i
            else:
                rows, lead = pl.ds((i % per) * block, block), i // per
            dense[lead, rows, j * block:(j + 1) * block] = piece
            flipped[lead, j * block:(j + 1) * block, rows] = piece.T

    fetch_values.wait()
    half = row_blocks // 2
    each(half, place)
    each(row.outer - 1, lambda k: xs.relay(0, k))
    each(row_blocks - half, lambda k: place(half + k))
    for h in range(1, PARTS):
        each(row.outer - 1, lambda k: xs.relay(h, k))

    agg = Scatter(col, c_near, c_near_in, c_far, c_far_in, c_total, (c_ns, c_nl, c_fs, c_fl))

    def forward(h, index):
        return dot(dense[index], xg[h].reshape(rows_n * own, width))

    for h in range(PARTS):
        if row.inner == 2:
            each(row.outer, lambda k: xs.passed(h, k))
        agg.start(h, forward)
    fetch_weight.wait()
    wcopy[...] = wide[...].astype(BF16)
    for h in range(PARTS):
        agg.middle(h, forward)
    for h in range(PARTS):
        span = slice(h * width, (h + 1) * width)
        part = agg.end(h).astype(BF16)
        mixed[:, span] = part
        term = dot(part, wcopy[span, :])
        activated[...] = term if h == 0 else activated[...] + term
    mixed16 = mixed[...]

    slopes = Chain(col, sg, sg_sent, sg_landed)
    for h in range(PARTS):
        span = slice(h * width, (h + 1) * width)
        total = activated[:, span]
        sigma = jax.nn.sigmoid(total)
        slope = cotangent[:, span].astype(F32) * (sigma * (1.0 + total * (1.0 - sigma)))
        sg[h, c] = slope.astype(BF16)
        slopes.start(h)
        activated[:, span] = total * sigma

    share = hidden // rows_n
    for h in range(PARTS):
        span = slice(h * width, (h + 1) * width)
        w1[:, :, span] = dot(mixed16, sg[h, c], 0, 0).reshape(rows_n, share, width).astype(BF16)

    def w1_copy(k):
        to = lax.rem(r + k + 1, rows_n)
        return remote(w1.at[to], w1_in.at[r], w1_sent.at[to], w1_landed.at[r], row.device(to))

    each(rows_n - 1, lambda k: w1_copy(k).start())

    def backward(h, index):
        return dot(flipped[index], sg[h, index])

    def add(h, index):
        grad[h] += backward(h, index)

    for h in range(PARTS):
        grad[h] = backward(h, c)
    each(col.outer - 1, lambda k: slopes.relay(k, range(PARTS), add))

    nodes = Scatter(row, e_near, e_near_in, e_far, e_far_in, e_total, (e_ns, e_nl, e_fs, e_fl))

    def term(h, index):
        return grad[h, pl.ds(pl.multiple_of(index * own, own), own), :]

    def w1_wait(k):
        source = lax.rem(r + rows_n - k - 1, rows_n)
        remote(w1.at[source], w1_in.at[source], w1_sent.at[source], w1_landed.at[source],
               row.device(source)).wait_recv()
        return source

    def w2_copy(k):
        to = lax.rem(c + k + 1, cols_n)
        return remote(w2.at[to], w2_in.at[c], w2_sent.at[to], w2_landed.at[c], col.device(to))

    def w2_wait(k):
        source = lax.rem(c + cols_n - k - 1, cols_n)
        remote(w2.at[source], w2_in.at[source], w2_sent.at[source], w2_landed.at[source],
               col.device(source)).wait_recv()

    for h in range(PARTS):
        if col.inner == 2:
            slopes.passed(-1, h, add)
            each(col.outer - 1, lambda k: slopes.passed(k, h, add))
        nodes.start(h, term)
        if h == 0:
            each(rows_n - 1, w1_wait)
            w1_in[r] = w1[r]
            weight_sum = jnp.sum(w1_in[...].astype(F32), axis=0)
            w2[...] = weight_sum.T.reshape(cols_n, hidden // cols_n, share).astype(w2.dtype)
            each(cols_n - 1, lambda k: w2_copy(k).start())
            w2_in[c] = w2[c]
        nodes.middle(h, term)

    out = None
    for h in range(PARTS):
        grad16 = nodes.end(h).astype(BF16)
        piece = dot(grad16, wcopy[:, h * width:(h + 1) * width], 1, 1)
        out = piece if out is None else out + piece
    dfeatures[...] = out

    each(cols_n - 1, w2_wait)
    dweight[...] = jnp.sum(w2_in[...].astype(F32), axis=0) * scale

    for h in range(PARTS):
        xs.drain(h)
        agg.drain(h)
        slopes.drain(h)
        nodes.drain(h)
    each(rows_n - 1, lambda k: w1_copy(k).wait_send())
    each(cols_n - 1, lambda k: w2_copy(k).wait_send())


def hand_over(a, b, c, a_out, b_out, c_out, a_held, b_held, c_held, sems):
    rows = ((a, a_held, a_out), (b, b_held, b_out), (c, c_held, c_out))
    ins = [pltpu.make_async_copy(src, held, sems.at[0, k]) for k, (src, held, _) in enumerate(rows)]
    outs = [pltpu.make_async_copy(held, dst, sems.at[1, k]) for k, (_, held, dst) in enumerate(rows)]
    for copy in ins:
        copy.start()
    for copy, after in zip(ins, outs):
        copy.wait()
        after.start()
    for copy in outs:
        copy.wait()


def on_device(rows_n, cols_n, features, weight, cotangent, block_values, block_coords):
    values, coords = block_values[0, 0], block_coords[0, 0]
    own, hidden = features.shape
    width = hidden // PARTS
    row_in, col_in = inner_size(rows_n), inner_size(cols_n)
    row_out, col_out = rows_n // row_in, cols_n // col_in
    scale = 1.0 / (own * rows_n * cols_n) ** 0.5
    share_r, share_c = hidden // rows_n, hidden // cols_n
    dma = pltpu.SemaphoreType.DMA

    def gather_scratch(count, outer):
        return [
            pltpu.VMEM((PARTS, count, own, width), BF16),
            dma((PARTS, 2 * outer)),
            dma((PARTS, count)),
        ]

    def scatter_scratch(outer):
        piece = pltpu.VMEM((PARTS, outer, own, width), BF16)
        return [piece] * 4 + [pltpu.VMEM((PARTS, own, width), F32)] + [dma((PARTS, outer))] * 4

    scratch = (
        gather_scratch(rows_n, row_out)
        + [
            pltpu.VMEM((cols_n, own, rows_n * own), BF16),
            pltpu.VMEM((cols_n, rows_n * own, own), BF16),
        ]
        + scatter_scratch(col_out)
        + [
            pltpu.VMEM((PARTS, cols_n, own, width), BF16),
            dma((PARTS, col_out, 3)),
            dma((PARTS, cols_n)),
        ]
        + [pltpu.VMEM((PARTS, rows_n * own, width), F32)]
        + scatter_scratch(row_out)
        + [pltpu.VMEM((rows_n, share_r, hidden), BF16)] * 2
        + [dma((rows_n,))] * 2
        + [pltpu.VMEM((cols_n, share_c, share_r), BF16)] * 2
        + [dma((cols_n,))] * 2
        + [
            pltpu.VMEM((hidden, hidden), BF16),
            pltpu.VMEM((hidden, hidden), F32),
            pltpu.VMEM((own, hidden), BF16),
            pltpu.VMEM((values.shape[0] + 1,) + values.shape[1:], BF16),
            dma((2,)),
        ]
    )
    vmem = pl.BlockSpec(memory_space=pltpu.VMEM)
    anywhere = pl.BlockSpec(memory_space=pl.ANY)
    results = pl.pallas_call(
        functools.partial(kernel, rows_n, cols_n, scale),
        out_shape=(
            jax.ShapeDtypeStruct((own, hidden), F32),
            jax.ShapeDtypeStruct((own, hidden), F32),
            jax.ShapeDtypeStruct((share_c, share_r), F32),
        ),
        in_specs=[pl.BlockSpec(memory_space=pltpu.SMEM), vmem, anywhere, vmem, anywhere],
        out_specs=(vmem, vmem, vmem),
        scratch_shapes=scratch,
        compiler_params=pltpu.CompilerParams(
            collective_id=0, has_side_effects=True, vmem_limit_bytes=56 * 1024 * 1024
        ),
    )(coords, features, weight, cotangent, values)
    ours, theirs, turned = pl.pallas_call(
        hand_over,
        out_shape=tuple(jax.ShapeDtypeStruct(a.shape, a.dtype) for a in results),
        in_specs=[pl.BlockSpec(memory_space=pltpu.HBM)] * 3,
        out_specs=(pl.BlockSpec(memory_space=pltpu.HBM),) * 3,
        scratch_shapes=[pltpu.VMEM(a.shape, a.dtype) for a in results] + [dma((2, 3))],
        compiler_params=pltpu.CompilerParams(vmem_limit_bytes=60 * 1024 * 1024),
    )(*results)
    return ours, theirs, turned.T


def solution(mesh):
    placed = (
        P(("col", "row"), None),
        P(),
        P(("row", "col"), None),
        P("row", "col", None, None, None),
        P("row", "col", None, None),
    )
    return jax.shard_map(
        functools.partial(on_device, mesh.shape["row"], mesh.shape["col"]),
        mesh=mesh,
        in_specs=placed,
        out_specs=(P(("row", "col"), None), P(("col", "row"), None), P("row", "col")),
        check_vma=False,
    )
```

```python
import functools

import jax
import jax.numpy as jnp
from jax import lax
from jax.experimental import pallas as pl
from jax.experimental.pallas import tpu as pltpu
from jax.sharding import PartitionSpec as P

MESH = pl.DeviceIdType.MESH
PARTS = 4
F32, BF16 = jnp.float32, jnp.bfloat16


def each(count, body):
    if count <= 8:
        for k in range(count):
            body(k)
    else:
        lax.fori_loop(0, count, lambda k, carry: (body(k), carry)[1], 0)


def inner_size(count):
    return 2 if count % 2 == 0 else 1


def dot(a, b, left=1, right=0):
    return lax.dot_general(a, b, (((left,), (right,)), ((), ())), preferred_element_type=F32)


def remote(src, dst, sent, landed, device):
    return pltpu.make_async_remote_copy(
        src_ref=src, dst_ref=dst, send_sem=sent, recv_sem=landed, device_id=device, device_id_type=MESH
    )


class Line:
    def __init__(self, name, count, device):
        self.count, self.device = count, device
        self.inner = inner_size(count)
        self.outer = count // self.inner
        self.me = lax.axis_index(name)
        self.o = self.me // self.inner
        self.i = self.me % self.inner

    def ahead(self, k):
        return lax.rem(self.o + k + 1, self.outer)

    def behind(self, k):
        return lax.rem(self.o + self.outer - k - 1, self.outer)

    def mate(self):
        return self.device(self.o * self.inner + 1 - self.i)


class Gather:
    def __init__(self, line, buf, sent, landed):
        self.line, self.buf, self.sent, self.landed = line, buf, sent, landed

    def copy(self, h, index, slot, device):
        piece = self.buf.at[h, index]
        return remote(piece, piece, self.sent.at[h, slot], self.landed.at[h, index], device)

    def start(self, h):
        line = self.line

        def far(k):
            self.copy(h, line.me, k, line.device(line.ahead(k) * line.inner + line.i)).start()

        if line.inner == 2:
            self.copy(h, line.me, line.outer - 1, line.mate()).start()
        each(line.outer - 1, far)

    def any_peer(self):
        line = self.line
        return line.device(lax.rem(line.me + 1, line.count))

    def relay(self, h, k):
        line = self.line
        index = line.behind(k) * line.inner + line.i
        self.copy(h, index, k, self.any_peer()).wait_recv()
        if line.inner == 2:
            self.copy(h, index, line.outer + k, line.mate()).start()
        return index

    def passed(self, h, k):
        line = self.line
        index = line.behind(k - 1) * line.inner + 1 - line.i
        self.copy(h, index, 0, self.any_peer()).wait_recv()
        return index

    def drain(self, h):
        line = self.line
        slots = 2 * line.outer - 1 if line.inner == 2 else line.outer - 1
        each(slots, lambda k: self.copy(h, line.me, k, self.any_peer()).wait_send())


class Chain:
    def __init__(self, line, buf, sent, landed):
        self.line, self.buf, self.sent, self.landed = line, buf, sent, landed

    def copy(self, h, index, way, device):
        piece = self.buf.at[h, index]
        return remote(
            piece, piece, self.sent.at[h, index // self.line.inner, way], self.landed.at[h, index], device
        )

    def side(self, way):
        line = self.line
        step = 1 if way == 0 else -1
        there = line.o + step
        inside = there < line.outer if way == 0 else there >= 0
        device = line.device(lax.rem(there + line.outer, line.outer) * line.inner + line.i)
        return inside, device

    def spread(self, h, index, ways):
        for way in ways:
            inside, device = self.side(way)

            @pl.when(inside)
            def _():
                self.copy(h, index, way, device).start()

        if self.line.inner == 2:
            self.copy(h, index, 2, self.line.mate()).start()

    def start(self, h):
        self.spread(h, self.line.me, (0, 1))

    def other(self):
        line = self.line
        return line.device(lax.rem(line.me + 1, line.count))

    def each_source(self, k, body):
        line = self.line
        for way, source in ((0, line.o - 1 - k), (1, line.o + 1 + k)):
            pl.when(jnp.logical_and(source >= 0, source < line.outer))(
                functools.partial(body, way, source))

    def relay(self, k, hidden_parts, use):
        def arrived(way, source):
            index = source * self.line.inner + self.line.i
            for h in hidden_parts:
                self.copy(h, index, way, self.other()).wait_recv()
                self.spread(h, index, (way,))
            for h in hidden_parts:
                use(h, index)

        self.each_source(k, arrived)

    def passed(self, k, h, use):
        def arrived(way, source):
            index = source * self.line.inner + 1 - self.line.i
            self.copy(h, index, 2, self.other()).wait_recv()
            use(h, index)

        if isinstance(k, int) and k < 0:
            arrived(2, self.line.o)
        else:
            self.each_source(k, arrived)

    def drain(self, h):
        line = self.line

        def one(source):
            index = source * line.inner + line.i
            for way in (0, 1):
                inside, device = self.side(way)
                went = source <= line.o if way == 0 else source >= line.o

                @pl.when(jnp.logical_and(inside, went))
                def _():
                    self.copy(h, index, way, device).wait_send()

            if line.inner == 2:
                self.copy(h, index, 2, line.mate()).wait_send()

        each(line.outer, one)


class Scatter:
    def __init__(self, line, near, near_in, far, far_in, total, sems):
        self.line, self.total = line, total
        self.near, self.near_in, self.far, self.far_in = near, near_in, far, far_in
        self.near_sent, self.near_landed, self.far_sent, self.far_landed = sems

    def near_copy(self, h, o2):
        return remote(
            self.near.at[h, o2], self.near_in.at[h, o2], self.near_sent.at[h, o2],
            self.near_landed.at[h, o2], self.line.mate(),
        )

    def far_copy(self, h, o2, source):
        return remote(
            self.far.at[h, o2], self.far_in.at[h, source], self.far_sent.at[h, o2],
            self.far_landed.at[h, source], self.line.device(o2 * self.line.inner + self.line.i),
        )

    def start(self, h, partial):
        line = self.line

        def one(k):
            o2 = line.ahead(k)
            self.near[h, o2] = partial(h, o2 * line.inner + 1 - line.i).astype(BF16)
            self.near_copy(h, o2).start()

        if line.inner == 2:
            each(line.outer, one)

    def pair(self, h, o2, partial):
        line = self.line
        value = partial(h, o2 * line.inner + line.i)
        if line.inner == 2:
            self.near_copy(h, o2).wait_recv()
            value = value + self.near_in[h, o2].astype(F32)
        return value

    def middle(self, h, partial):
        line = self.line

        def one(k):
            o2 = line.ahead(k)
            self.far[h, o2] = self.pair(h, o2, partial).astype(BF16)
            self.far_copy(h, o2, line.o).start()

        each(line.outer - 1, one)
        self.total[h] = self.pair(h, line.o, partial)

    def end(self, h):
        line = self.line

        def one(k):
            source = line.behind(k)
            self.far_copy(h, line.ahead(0), source).wait_recv()
            self.total[h] += self.far_in[h, source].astype(F32)

        each(line.outer - 1, one)
        return self.total[h]

    def drain(self, h):
        line = self.line
        if line.inner == 2:
            each(line.outer, lambda k: self.near_copy(h, k).wait_send())
        each(line.outer - 1, lambda k: self.far_copy(h, line.ahead(k), line.o).wait_send())


def kernel(
    rows_n, cols_n, scale,
    coords, features, weight, cotangent, values,
    activated, dfeatures, dweight,
    xg, xg_sent, xg_landed,
    dense, flipped,
    c_near, c_near_in, c_far, c_far_in, c_total, c_ns, c_nl, c_fs, c_fl,
    sg, sg_sent, sg_landed,
    grad,
    e_near, e_near_in, e_far, e_far_in, e_total, e_ns, e_nl, e_fs, e_fl,
    w1, w1_in, w1_sent, w1_landed,
    w2, w2_in, w2_sent, w2_landed,
    wcopy, wide, mixed, stock, fetched,
):
    r, c = lax.axis_index("row"), lax.axis_index("col")
    row = Line("row", rows_n, lambda index: (index, c))
    col = Line("col", cols_n, lambda index: (r, index))
    own, hidden = features.shape
    width = hidden // PARTS
    slots, block = values.shape[0], values.shape[1]

    barrier = pltpu.get_barrier_semaphore()
    each(rows_n - 1, lambda k: pl.semaphore_signal(
        barrier, inc=1, device_id=row.device(lax.rem(r + k + 1, rows_n)), device_id_type=MESH))
    each(cols_n - 1, lambda k: pl.semaphore_signal(
        barrier, inc=1, device_id=col.device(lax.rem(c + k + 1, cols_n)), device_id_type=MESH))
    fetch_values = pltpu.make_async_copy(values, stock.at[pl.ds(0, slots)], fetched.at[0])
    fetch_weight = pltpu.make_async_copy(weight, wide, fetched.at[1])
    fetch_values.start()
    fetch_weight.start()
    for h in range(PARTS):
        xg[h, r] = features[:, h * width:(h + 1) * width].astype(BF16)
    stock[slots] = jnp.zeros((block, block), BF16)
    pl.semaphore_wait(barrier, rows_n + cols_n - 2)

    xs = Gather(row, xg, xg_sent, xg_landed)
    for h in range(PARTS):
        xs.start(h)

    row_blocks, col_blocks = cols_n * own // block, rows_n * own // block
    per = own // block
    short = slots <= 16
    keys = [coords[0, s] * col_blocks + coords[1, s] for s in range(slots)] if short else None

    def place(i):
        for j in range(col_blocks):
            def look(s, found):
                key = keys[s] if short else coords[0, s] * col_blocks + coords[1, s]
                return jnp.where(key == i * col_blocks + j, s, found)

            found = jnp.int32(slots)
            if short:
                for s in range(slots):
                    found = look(s, found)
            else:
                found = lax.fori_loop(0, slots, look, found)
            piece = stock[found]
            if per == 1:
                rows, lead = pl.ds(0, block), i
            else:
                rows, lead = pl.ds((i % per) * block, block), i // per
            dense[lead, rows, j * block:(j + 1) * block] = piece
            flipped[lead, j * block:(j + 1) * block, rows] = piece.T

    fetch_values.wait()
    half = row_blocks // 2
    each(half, place)
    each(row.outer - 1, lambda k: xs.relay(0, k))
    each(row_blocks - half, lambda k: place(half + k))
    for h in range(1, PARTS):
        each(row.outer - 1, lambda k: xs.relay(h, k))

    agg = Scatter(col, c_near, c_near_in, c_far, c_far_in, c_total, (c_ns, c_nl, c_fs, c_fl))

    def forward(h, index):
        return dot(dense[index], xg[h].reshape(rows_n * own, width))

    for h in range(PARTS):
        if row.inner == 2:
            each(row.outer, lambda k: xs.passed(h, k))
        agg.start(h, forward)
    fetch_weight.wait()
    wcopy[...] = wide[...].astype(BF16)
    for h in range(PARTS):
        agg.middle(h, forward)
    for h in range(PARTS):
        span = slice(h * width, (h + 1) * width)
        part = agg.end(h).astype(BF16)
        mixed[:, span] = part
        term = dot(part, wcopy[span, :])
        activated[...] = term if h == 0 else activated[...] + term
    mixed16 = mixed[...]

    slopes = Chain(col, sg, sg_sent, sg_landed)
    for h in range(PARTS):
        span = slice(h * width, (h + 1) * width)
        total = activated[:, span]
        sigma = jax.nn.sigmoid(total)
        slope = cotangent[:, span].astype(F32) * (sigma * (1.0 + total * (1.0 - sigma)))
        sg[h, c] = slope.astype(BF16)
        slopes.start(h)
        activated[:, span] = total * sigma

    share = hidden // rows_n
    for h in range(PARTS):
        span = slice(h * width, (h + 1) * width)
        w1[:, :, span] = dot(mixed16, sg[h, c], 0, 0).reshape(rows_n, share, width).astype(BF16)

    def w1_copy(k):
        to = lax.rem(r + k + 1, rows_n)
        return remote(w1.at[to], w1_in.at[r], w1_sent.at[to], w1_landed.at[r], row.device(to))

    each(rows_n - 1, lambda k: w1_copy(k).start())

    def backward(h, index):
        return dot(flipped[index], sg[h, index])

    def add(h, index):
        grad[h] += backward(h, index)

    for h in range(PARTS):
        grad[h] = backward(h, c)
    each(col.outer - 1, lambda k: slopes.relay(k, range(PARTS), add))

    nodes = Scatter(row, e_near, e_near_in, e_far, e_far_in, e_total, (e_ns, e_nl, e_fs, e_fl))

    def term(h, index):
        return grad[h, pl.ds(pl.multiple_of(index * own, own), own), :]

    def w1_wait(k):
        source = lax.rem(r + rows_n - k - 1, rows_n)
        remote(w1.at[source], w1_in.at[source], w1_sent.at[source], w1_landed.at[source],
               row.device(source)).wait_recv()
        return source

    def w2_copy(k):
        to = lax.rem(c + k + 1, cols_n)
        return remote(w2.at[to], w2_in.at[c], w2_sent.at[to], w2_landed.at[c], col.device(to))

    def w2_wait(k):
        source = lax.rem(c + cols_n - k - 1, cols_n)
        remote(w2.at[source], w2_in.at[source], w2_sent.at[source], w2_landed.at[source],
               col.device(source)).wait_recv()

    for h in range(PARTS):
        if col.inner == 2:
            slopes.passed(-1, h, add)
            each(col.outer - 1, lambda k: slopes.passed(k, h, add))
        nodes.start(h, term)
        if h == 0:
            each(rows_n - 1, w1_wait)
            w1_in[r] = w1[r]
            weight_sum = jnp.sum(w1_in[...].astype(F32), axis=0)
            w2[...] = weight_sum.T.reshape(cols_n, hidden // cols_n, share).astype(w2.dtype)
            each(cols_n - 1, lambda k: w2_copy(k).start())
            w2_in[c] = w2[c]
        nodes.middle(h, term)

    out = None
    for h in range(PARTS):
        grad16 = nodes.end(h).astype(BF16)
        piece = dot(grad16, wcopy[:, h * width:(h + 1) * width], 1, 1)
        out = piece if out is None else out + piece
    dfeatures[...] = out

    each(cols_n - 1, w2_wait)
    dweight[...] = jnp.sum(w2_in[...].astype(F32), axis=0) * scale

    for h in range(PARTS):
        xs.drain(h)
        agg.drain(h)
        slopes.drain(h)
        nodes.drain(h)
    each(rows_n - 1, lambda k: w1_copy(k).wait_send())
    each(cols_n - 1, lambda k: w2_copy(k).wait_send())


def hand_over(a, b, c, a_out, b_out, c_out, a_held, b_held, c_held, sems):
    rows = ((a, a_held, a_out), (b, b_held, b_out), (c, c_held, c_out))
    ins = [pltpu.make_async_copy(src, held, sems.at[0, k]) for k, (src, held, _) in enumerate(rows)]
    outs = [pltpu.make_async_copy(held, dst, sems.at[1, k]) for k, (_, held, dst) in enumerate(rows)]
    for copy in ins:
        copy.start()
    for copy, after in zip(ins, outs):
        copy.wait()
        after.start()
    for copy in outs:
        copy.wait()


def on_device(rows_n, cols_n, features, weight, cotangent, block_values, block_coords):
    values, coords = block_values[0, 0], block_coords[0, 0]
    own, hidden = features.shape
    width = hidden // PARTS
    row_in, col_in = inner_size(rows_n), inner_size(cols_n)
    row_out, col_out = rows_n // row_in, cols_n // col_in
    scale = 1.0 / (own * rows_n * cols_n) ** 0.5
    share_r, share_c = hidden // rows_n, hidden // cols_n
    dma = pltpu.SemaphoreType.DMA

    def gather_scratch(count, outer):
        return [
            pltpu.VMEM((PARTS, count, own, width), BF16),
            dma((PARTS, 2 * outer)),
            dma((PARTS, count)),
        ]

    def scatter_scratch(outer):
        piece = pltpu.VMEM((PARTS, outer, own, width), BF16)
        return [piece] * 4 + [pltpu.VMEM((PARTS, own, width), F32)] + [dma((PARTS, outer))] * 4

    scratch = (
        gather_scratch(rows_n, row_out)
        + [
            pltpu.VMEM((cols_n, own, rows_n * own), BF16),
            pltpu.VMEM((cols_n, rows_n * own, own), BF16),
        ]
        + scatter_scratch(col_out)
        + [
            pltpu.VMEM((PARTS, cols_n, own, width), BF16),
            dma((PARTS, col_out, 3)),
            dma((PARTS, cols_n)),
        ]
        + [pltpu.VMEM((PARTS, rows_n * own, width), F32)]
        + scatter_scratch(row_out)
        + [pltpu.VMEM((rows_n, share_r, hidden), BF16)] * 2
        + [dma((rows_n,))] * 2
        + [pltpu.VMEM((cols_n, share_c, share_r), BF16)] * 2
        + [dma((cols_n,))] * 2
        + [
            pltpu.VMEM((hidden, hidden), BF16),
            pltpu.VMEM((hidden, hidden), F32),
            pltpu.VMEM((own, hidden), BF16),
            pltpu.VMEM((values.shape[0] + 1,) + values.shape[1:], BF16),
            dma((2,)),
        ]
    )
    vmem = pl.BlockSpec(memory_space=pltpu.VMEM)
    anywhere = pl.BlockSpec(memory_space=pl.ANY)
    results = pl.pallas_call(
        functools.partial(kernel, rows_n, cols_n, scale),
        out_shape=(
            jax.ShapeDtypeStruct((own, hidden), F32),
            jax.ShapeDtypeStruct((own, hidden), F32),
            jax.ShapeDtypeStruct((share_c, share_r), F32),
        ),
        in_specs=[pl.BlockSpec(memory_space=pltpu.SMEM), vmem, anywhere, vmem, anywhere],
        out_specs=(vmem, vmem, vmem),
        scratch_shapes=scratch,
        compiler_params=pltpu.CompilerParams(
            collective_id=0, has_side_effects=True, vmem_limit_bytes=56 * 1024 * 1024
        ),
    )(coords, features, weight, cotangent, values)
    ours, theirs, turned = pl.pallas_call(
        hand_over,
        out_shape=tuple(jax.ShapeDtypeStruct(a.shape, a.dtype) for a in results),
        in_specs=[pl.BlockSpec(memory_space=pltpu.HBM)] * 3,
        out_specs=(pl.BlockSpec(memory_space=pltpu.HBM),) * 3,
        scratch_shapes=[pltpu.VMEM(a.shape, a.dtype) for a in results] + [dma((2, 3))],
        compiler_params=pltpu.CompilerParams(vmem_limit_bytes=60 * 1024 * 1024),
    )(*results)
    return ours, theirs, turned.T


def solution(mesh):
    placed = (
        P(("col", "row"), None),
        P(),
        P(("row", "col"), None),
        P("row", "col", None, None, None),
        P("row", "col", None, None),
    )
    return jax.shard_map(
        functools.partial(on_device, mesh.shape["row"], mesh.shape["col"]),
        mesh=mesh,
        in_specs=placed,
        out_specs=(P(("row", "col"), None), P(("col", "row"), None), P("row", "col")),
        check_vma=False,
    )
```

```python
import functools

import jax
import jax.numpy as jnp
from jax import lax
from jax.experimental import pallas as pl
from jax.experimental.pallas import tpu as pltpu
from jax.sharding import PartitionSpec as P

MESH = pl.DeviceIdType.MESH
PARTS = 2
F32, BF16 = jnp.float32, jnp.bfloat16


def each(count, body):
    if count <= 8:
        for k in range(count):
            body(k)
    else:
        lax.fori_loop(0, count, lambda k, carry: (body(k), carry)[1], 0)


def inner_size(count):
    return 2 if count % 2 == 0 else 1


def dot(a, b, left=1, right=0):
    return lax.dot_general(a, b, (((left,), (right,)), ((), ())), preferred_element_type=F32)


def remote(src, dst, sent, landed, device):
    return pltpu.make_async_remote_copy(
        src_ref=src, dst_ref=dst, send_sem=sent, recv_sem=landed, device_id=device, device_id_type=MESH
    )


class Line:
    def __init__(self, name, count, device):
        self.count, self.device = count, device
        self.inner = inner_size(count)
        self.outer = count // self.inner
        self.me = lax.axis_index(name)
        self.o = self.me // self.inner
        self.i = self.me % self.inner

    def ahead(self, k):
        return lax.rem(self.o + k + 1, self.outer)

    def behind(self, k):
        return lax.rem(self.o + self.outer - k - 1, self.outer)

    def mate(self):
        return self.device(self.o * self.inner + 1 - self.i)


class Gather:
    def __init__(self, line, buf, sent, landed):
        self.line, self.buf, self.sent, self.landed = line, buf, sent, landed

    def copy(self, h, index, slot, device):
        piece = self.buf.at[h, index]
        return remote(piece, piece, self.sent.at[h, slot], self.landed.at[h, index], device)

    def start(self, h):
        line = self.line

        def far(k):
            self.copy(h, line.me, k, line.device(line.ahead(k) * line.inner + line.i)).start()

        if line.inner == 2:
            self.copy(h, line.me, line.outer - 1, line.mate()).start()
        each(line.outer - 1, far)

    def any_peer(self):
        line = self.line
        return line.device(lax.rem(line.me + 1, line.count))

    def relay(self, h, k):
        line = self.line
        index = line.behind(k) * line.inner + line.i
        self.copy(h, index, k, self.any_peer()).wait_recv()
        if line.inner == 2:
            self.copy(h, index, line.outer + k, line.mate()).start()
        return index

    def passed(self, h, k):
        line = self.line
        index = line.behind(k - 1) * line.inner + 1 - line.i
        self.copy(h, index, 0, self.any_peer()).wait_recv()
        return index

    def drain(self, h):
        line = self.line
        slots = 2 * line.outer - 1 if line.inner == 2 else line.outer - 1
        each(slots, lambda k: self.copy(h, line.me, k, self.any_peer()).wait_send())


class Chain:
    def __init__(self, line, buf, sent, landed):
        self.line, self.buf, self.sent, self.landed = line, buf, sent, landed

    def copy(self, h, index, way, device):
        piece = self.buf.at[h, index]
        return remote(
            piece, piece, self.sent.at[h, index // self.line.inner, way], self.landed.at[h, index], device
        )

    def side(self, way):
        line = self.line
        step = 1 if way == 0 else -1
        there = line.o + step
        inside = there < line.outer if way == 0 else there >= 0
        device = line.device(lax.rem(there + line.outer, line.outer) * line.inner + line.i)
        return inside, device

    def spread(self, h, index, ways):
        for way in ways:
            inside, device = self.side(way)

            @pl.when(inside)
            def _():
                self.copy(h, index, way, device).start()

        if self.line.inner == 2:
            self.copy(h, index, 2, self.line.mate()).start()

    def start(self, h):
        self.spread(h, self.line.me, (0, 1))

    def other(self):
        line = self.line
        return line.device(lax.rem(line.me + 1, line.count))

    def each_source(self, k, body):
        line = self.line
        for way, source in ((0, line.o - 1 - k), (1, line.o + 1 + k)):
            pl.when(jnp.logical_and(source >= 0, source < line.outer))(
                functools.partial(body, way, source))

    def relay(self, k, h, use):
        def arrived(way, source):
            index = source * self.line.inner + self.line.i
            self.copy(h, index, way, self.other()).wait_recv()
            self.spread(h, index, (way,))
            if use is not None:
                use(index)

        self.each_source(k, arrived)

    def passed(self, k, h, use):
        def arrived(way, source):
            index = source * self.line.inner + 1 - self.line.i
            self.copy(h, index, 2, self.other()).wait_recv()
            if use is not None:
                use(index)

        if isinstance(k, int) and k < 0:
            arrived(2, self.line.o)
        else:
            self.each_source(k, arrived)

    def drain(self, h):
        line = self.line

        def one(source):
            index = source * line.inner + line.i
            for way in (0, 1):
                inside, device = self.side(way)
                went = source <= line.o if way == 0 else source >= line.o

                @pl.when(jnp.logical_and(inside, went))
                def _():
                    self.copy(h, index, way, device).wait_send()

            if line.inner == 2:
                self.copy(h, index, 2, line.mate()).wait_send()

        each(line.outer, one)


class Scatter:
    def __init__(self, line, near, near_in, far, far_in, total, sems):
        self.line, self.total = line, total
        self.near, self.near_in, self.far, self.far_in = near, near_in, far, far_in
        self.near_sent, self.near_landed, self.far_sent, self.far_landed = sems

    def near_copy(self, h, o2):
        return remote(
            self.near.at[h, o2], self.near_in.at[h, o2], self.near_sent.at[h, o2],
            self.near_landed.at[h, o2], self.line.mate(),
        )

    def far_copy(self, h, o2, source):
        return remote(
            self.far.at[h, o2], self.far_in.at[h, source], self.far_sent.at[h, o2],
            self.far_landed.at[h, source], self.line.device(o2 * self.line.inner + self.line.i),
        )

    def start(self, h, partial):
        line = self.line

        def one(k):
            o2 = line.ahead(k)
            self.near[h, o2] = partial(h, o2 * line.inner + 1 - line.i).astype(BF16)
            self.near_copy(h, o2).start()

        if line.inner == 2:
            each(line.outer, one)

    def pair(self, h, o2, partial):
        line = self.line
        value = partial(h, o2 * line.inner + line.i)
        if line.inner == 2:
            self.near_copy(h, o2).wait_recv()
            value = value + self.near_in[h, o2].astype(F32)
        return value

    def middle(self, h, partial, first, last):
        line = self.line

        def one(k):
            o2 = line.ahead(first + k)
            self.far[h, o2] = self.pair(h, o2, partial).astype(BF16)
            self.far_copy(h, o2, line.o).start()

        each(last - first, one)
        if last == line.outer - 1:
            self.total[h] = self.pair(h, line.o, partial)

    def end(self, h):
        line = self.line

        def one(k):
            source = line.behind(k)
            self.far_copy(h, line.ahead(0), source).wait_recv()
            self.total[h] += self.far_in[h, source].astype(F32)

        each(line.outer - 1, one)
        return self.total[h]

    def drain(self, h):
        line = self.line
        if line.inner == 2:
            each(line.outer, lambda k: self.near_copy(h, k).wait_send())
        each(line.outer - 1, lambda k: self.far_copy(h, line.ahead(k), line.o).wait_send())


def kernel(
    rows_n, cols_n, scale,
    coords, features, weight, cotangent, values,
    activated, dfeatures, dweight,
    xg, xg_sent, xg_landed,
    dense, flipped,
    c_near, c_near_in, c_far, c_far_in, c_total, c_ns, c_nl, c_fs, c_fl,
    sg, sg_sent, sg_landed,
    grad,
    e_near, e_near_in, e_far, e_far_in, e_total, e_ns, e_nl, e_fs, e_fl,
    w1, w1_in, w1_sent, w1_landed,
    w2, w2_in, w2_sent, w2_landed,
    wcopy, wide, mixed, stock, fetched,
):
    r, c = lax.axis_index("row"), lax.axis_index("col")
    row = Line("row", rows_n, lambda index: (index, c))
    col = Line("col", cols_n, lambda index: (r, index))
    own, hidden = features.shape
    width = hidden // PARTS
    slots, block = values.shape[0], values.shape[1]

    barrier = pltpu.get_barrier_semaphore()
    each(rows_n - 1, lambda k: pl.semaphore_signal(
        barrier, inc=1, device_id=row.device(lax.rem(r + k + 1, rows_n)), device_id_type=MESH))
    each(cols_n - 1, lambda k: pl.semaphore_signal(
        barrier, inc=1, device_id=col.device(lax.rem(c + k + 1, cols_n)), device_id_type=MESH))
    fetch_values = pltpu.make_async_copy(values, stock.at[pl.ds(0, slots)], fetched.at[0])
    fetch_weight = pltpu.make_async_copy(weight, wide, fetched.at[1])
    fetch_values.start()
    fetch_weight.start()
    for h in range(PARTS):
        xg[h, r] = features[:, h * width:(h + 1) * width].astype(BF16)
    stock[slots] = jnp.zeros((block, block), BF16)
    pl.semaphore_wait(barrier, rows_n + cols_n - 2)

    xs = Gather(row, xg, xg_sent, xg_landed)
    for h in range(PARTS):
        xs.start(h)

    row_blocks, col_blocks = cols_n * own // block, rows_n * own // block
    per = own // block
    short = slots <= 16
    keys = [coords[0, s] * col_blocks + coords[1, s] for s in range(slots)] if short else None

    def place(i):
        for j in range(col_blocks):
            def look(s, found):
                key = keys[s] if short else coords[0, s] * col_blocks + coords[1, s]
                return jnp.where(key == i * col_blocks + j, s, found)

            found = jnp.int32(slots)
            if short:
                for s in range(slots):
                    found = look(s, found)
            else:
                found = lax.fori_loop(0, slots, look, found)
            piece = stock[found]
            if per == 1:
                rows, lead = pl.ds(0, block), i
            else:
                rows, lead = pl.ds((i % per) * block, block), i // per
            dense[lead, rows, j * block:(j + 1) * block] = piece
            flipped[lead, j * block:(j + 1) * block, rows] = piece.T

    fetch_values.wait()
    half = row_blocks // 2
    each(half, place)
    each(row.outer - 1, lambda k: xs.relay(0, k))
    each(row_blocks - half, lambda k: place(half + k))
    for h in range(1, PARTS):
        each(row.outer - 1, lambda k: xs.relay(h, k))

    agg = Scatter(col, c_near, c_near_in, c_far, c_far_in, c_total, (c_ns, c_nl, c_fs, c_fl))

    tall = own // PARTS

    def forward(p, index):
        rows = dense[index, p * tall:(p + 1) * tall, :]
        return jnp.concatenate(
            [dot(rows, xg[h].reshape(rows_n * own, width)) for h in range(PARTS)], axis=1)

    for h in range(PARTS):
        if row.inner == 2:
            each(row.outer, lambda k: xs.passed(h, k))
    for p in range(PARTS):
        agg.start(p, forward)
    fetch_weight.wait()
    wcopy[...] = wide[...].astype(BF16)

    slopes = Chain(col, sg, sg_sent, sg_landed)

    def own_slope(p):
        span = slice(p * tall, (p + 1) * tall)
        part = agg.end(p).astype(BF16)
        total = dot(part, wcopy[...])
        sigma = jax.nn.sigmoid(total)
        slope = cotangent[span, :].astype(F32) * (sigma * (1.0 + total * (1.0 - sigma)))
        sg[p, c] = slope.astype(BF16)
        slopes.start(p)
        mixed[span, :] = part
        activated[span, :] = total * sigma

    hops = col.outer - 1
    for p in range(PARTS):
        early = (hops + 1) // 2 if p else hops
        agg.middle(p, forward, 0, early)
        if p:
            own_slope(p - 1)
            agg.middle(p, forward, early, hops)
            each(min(hops, 1), lambda k: slopes.relay(k, p - 1, None))
    own_slope(PARTS - 1)

    def both(index):
        return jnp.concatenate([sg[p, index] for p in range(PARTS)], axis=0)

    share = hidden // rows_n
    w1[...] = dot(mixed[...], both(c), 0, 0).reshape(rows_n, share, hidden).astype(BF16)

    def w1_copy(k):
        to = lax.rem(r + k + 1, rows_n)
        return remote(w1.at[to], w1_in.at[r], w1_sent.at[to], w1_landed.at[r], row.device(to))

    each(rows_n - 1, lambda k: w1_copy(k).start())

    def backward(h, index):
        return dot(flipped[index], both(index)[:, h * width:(h + 1) * width])

    def add(index):
        for h in range(PARTS):
            grad[h] += backward(h, index)

    for p in range(PARTS):
        seen = min(hops, 1) if p < PARTS - 1 else 0
        each(hops - seen, lambda k: slopes.relay(seen + k, p, add if p == PARTS - 1 else None))
        if p == 0:
            for h in range(PARTS):
                grad[h] = backward(h, c)

    nodes = Scatter(row, e_near, e_near_in, e_far, e_far_in, e_total, (e_ns, e_nl, e_fs, e_fl))

    def term(h, index):
        return grad[h, pl.ds(pl.multiple_of(index * own, own), own), :]

    def w1_wait(k):
        source = lax.rem(r + rows_n - k - 1, rows_n)
        remote(w1.at[source], w1_in.at[source], w1_sent.at[source], w1_landed.at[source],
               row.device(source)).wait_recv()
        return source

    def w2_copy(k):
        to = lax.rem(c + k + 1, cols_n)
        return remote(w2.at[to], w2_in.at[c], w2_sent.at[to], w2_landed.at[c], col.device(to))

    def w2_wait(k):
        source = lax.rem(c + cols_n - k - 1, cols_n)
        remote(w2.at[source], w2_in.at[source], w2_sent.at[source], w2_landed.at[source],
               col.device(source)).wait_recv()

    each(rows_n - 1, w1_wait)
    w1_in[r] = w1[r]
    weight_sum = jnp.sum(w1_in[...].astype(F32), axis=0)
    w2[...] = weight_sum.T.reshape(cols_n, hidden // cols_n, share).astype(w2.dtype)
    each(cols_n - 1, lambda k: w2_copy(k).start())
    w2_in[c] = w2[c]

    for p in range(PARTS):
        if col.inner == 2:
            use = add if p == PARTS - 1 else None
            slopes.passed(-1, p, use)
            each(hops, lambda k: slopes.passed(k, p, use))
    for h in range(PARTS):
        nodes.start(h, term)
    for h in range(PARTS):
        nodes.middle(h, term, 0, row.outer - 1)

    out = None
    for h in range(PARTS):
        grad16 = nodes.end(h).astype(BF16)
        piece = dot(grad16, wcopy[:, h * width:(h + 1) * width], 1, 1)
        out = piece if out is None else out + piece
    dfeatures[...] = out

    each(cols_n - 1, w2_wait)
    dweight[...] = jnp.sum(w2_in[...].astype(F32), axis=0) * scale

    for h in range(PARTS):
        xs.drain(h)
        agg.drain(h)
        slopes.drain(h)
        nodes.drain(h)
    each(rows_n - 1, lambda k: w1_copy(k).wait_send())
    each(cols_n - 1, lambda k: w2_copy(k).wait_send())


def hand_over(a, b, c, a_out, b_out, c_out, a_held, b_held, c_held, sems):
    rows = ((a, a_held, a_out), (b, b_held, b_out), (c, c_held, c_out))
    ins = [pltpu.make_async_copy(src, held, sems.at[0, k]) for k, (src, held, _) in enumerate(rows)]
    outs = [pltpu.make_async_copy(held, dst, sems.at[1, k]) for k, (_, held, dst) in enumerate(rows)]
    for copy in ins:
        copy.start()
    for copy, after in zip(ins, outs):
        copy.wait()
        after.start()
    for copy in outs:
        copy.wait()


def on_device(rows_n, cols_n, features, weight, cotangent, block_values, block_coords):
    values, coords = block_values[0, 0], block_coords[0, 0]
    own, hidden = features.shape
    width = hidden // PARTS
    row_in, col_in = inner_size(rows_n), inner_size(cols_n)
    row_out, col_out = rows_n // row_in, cols_n // col_in
    scale = 1.0 / (own * rows_n * cols_n) ** 0.5
    share_r, share_c = hidden // rows_n, hidden // cols_n
    dma = pltpu.SemaphoreType.DMA

    def gather_scratch(count, outer):
        return [
            pltpu.VMEM((PARTS, count, own, width), BF16),
            dma((PARTS, 2 * outer)),
            dma((PARTS, count)),
        ]

    def scatter_scratch(outer, piece):
        return (
            [pltpu.VMEM((PARTS, outer) + piece, BF16)] * 4
            + [pltpu.VMEM((PARTS,) + piece, F32)]
            + [dma((PARTS, outer))] * 4
        )

    scratch = (
        gather_scratch(rows_n, row_out)
        + [
            pltpu.VMEM((cols_n, own, rows_n * own), BF16),
            pltpu.VMEM((cols_n, rows_n * own, own), BF16),
        ]
        + scatter_scratch(col_out, (own // PARTS, hidden))
        + [
            pltpu.VMEM((PARTS, cols_n, own // PARTS, hidden), BF16),
            dma((PARTS, col_out, 3)),
            dma((PARTS, cols_n)),
        ]
        + [pltpu.VMEM((PARTS, rows_n * own, width), F32)]
        + scatter_scratch(row_out, (own, width))
        + [pltpu.VMEM((rows_n, share_r, hidden), BF16)] * 2
        + [dma((rows_n,))] * 2
        + [pltpu.VMEM((cols_n, share_c, share_r), BF16)] * 2
        + [dma((cols_n,))] * 2
        + [
            pltpu.VMEM((hidden, hidden), BF16),
            pltpu.VMEM((hidden, hidden), F32),
            pltpu.VMEM((own, hidden), BF16),
            pltpu.VMEM((values.shape[0] + 1,) + values.shape[1:], BF16),
            dma((2,)),
        ]
    )
    vmem = pl.BlockSpec(memory_space=pltpu.VMEM)
    anywhere = pl.BlockSpec(memory_space=pl.ANY)
    results = pl.pallas_call(
        functools.partial(kernel, rows_n, cols_n, scale),
        out_shape=(
            jax.ShapeDtypeStruct((own, hidden), F32),
            jax.ShapeDtypeStruct((own, hidden), F32),
            jax.ShapeDtypeStruct((share_c, share_r), F32),
        ),
        in_specs=[pl.BlockSpec(memory_space=pltpu.SMEM), vmem, anywhere, vmem, anywhere],
        out_specs=(vmem, vmem, vmem),
        scratch_shapes=scratch,
        compiler_params=pltpu.CompilerParams(
            collective_id=0, has_side_effects=True, vmem_limit_bytes=56 * 1024 * 1024
        ),
    )(coords, features, weight, cotangent, values)
    ours, theirs, turned = pl.pallas_call(
        hand_over,
        out_shape=tuple(jax.ShapeDtypeStruct(a.shape, a.dtype) for a in results),
        in_specs=[pl.BlockSpec(memory_space=pltpu.HBM)] * 3,
        out_specs=(pl.BlockSpec(memory_space=pltpu.HBM),) * 3,
        scratch_shapes=[pltpu.VMEM(a.shape, a.dtype) for a in results] + [dma((2, 3))],
        compiler_params=pltpu.CompilerParams(vmem_limit_bytes=60 * 1024 * 1024),
    )(*results)
    return ours, theirs, turned.T


def solution(mesh):
    placed = (
        P(("col", "row"), None),
        P(),
        P(("row", "col"), None),
        P("row", "col", None, None, None),
        P("row", "col", None, None),
    )
    return jax.shard_map(
        functools.partial(on_device, mesh.shape["row"], mesh.shape["col"]),
        mesh=mesh,
        in_specs=placed,
        out_specs=(P(("row", "col"), None), P(("col", "row"), None), P("row", "col")),
        check_vma=False,
    )
```

```python
import functools

import jax
import jax.numpy as jnp
from jax import lax
from jax.experimental import pallas as pl
from jax.experimental.pallas import tpu as pltpu
from jax.sharding import PartitionSpec as P

MESH = pl.DeviceIdType.MESH
PARTS = 2
F32, BF16 = jnp.float32, jnp.bfloat16


def each(count, body):
    if count <= 8:
        for k in range(count):
            body(k)
    else:
        lax.fori_loop(0, count, lambda k, carry: (body(k), carry)[1], 0)


def inner_size(count):
    return 2 if count % 2 == 0 else 1


def dot(a, b, left=1, right=0):
    return lax.dot_general(a, b, (((left,), (right,)), ((), ())), preferred_element_type=F32)


def remote(src, dst, sent, landed, device):
    return pltpu.make_async_remote_copy(
        src_ref=src, dst_ref=dst, send_sem=sent, recv_sem=landed, device_id=device, device_id_type=MESH
    )


class Line:
    def __init__(self, name, count, device):
        self.count, self.device = count, device
        self.inner = inner_size(count)
        self.outer = count // self.inner
        self.me = lax.axis_index(name)
        self.o = self.me // self.inner
        self.i = self.me % self.inner

    def ahead(self, k):
        return lax.rem(self.o + k + 1, self.outer)

    def behind(self, k):
        return lax.rem(self.o + self.outer - k - 1, self.outer)

    def mate(self):
        return self.device(self.o * self.inner + 1 - self.i)


class Gather:
    def __init__(self, line, buf, sent, landed):
        self.line, self.buf, self.sent, self.landed = line, buf, sent, landed

    def copy(self, h, index, slot, device):
        piece = self.buf.at[h, index]
        return remote(piece, piece, self.sent.at[h, slot], self.landed.at[h, index], device)

    def start(self, h):
        line = self.line

        def far(k):
            self.copy(h, line.me, k, line.device(line.ahead(k) * line.inner + line.i)).start()

        if line.inner == 2:
            self.copy(h, line.me, line.outer - 1, line.mate()).start()
        each(line.outer - 1, far)

    def any_peer(self):
        line = self.line
        return line.device(lax.rem(line.me + 1, line.count))

    def relay(self, h, k):
        line = self.line
        index = line.behind(k) * line.inner + line.i
        self.copy(h, index, k, self.any_peer()).wait_recv()
        if line.inner == 2:
            self.copy(h, index, line.outer + k, line.mate()).start()
        return index

    def passed(self, h, k):
        line = self.line
        index = line.behind(k - 1) * line.inner + 1 - line.i
        self.copy(h, index, 0, self.any_peer()).wait_recv()
        return index

    def drain(self, h):
        line = self.line
        slots = 2 * line.outer - 1 if line.inner == 2 else line.outer - 1
        each(slots, lambda k: self.copy(h, line.me, k, self.any_peer()).wait_send())


class Chain:
    def __init__(self, line, buf, sent, landed):
        self.line, self.buf, self.sent, self.landed = line, buf, sent, landed

    def copy(self, h, index, way, device):
        piece = self.buf.at[h, index]
        return remote(
            piece, piece, self.sent.at[h, index // self.line.inner, way], self.landed.at[h, index], device
        )

    def side(self, way):
        line = self.line
        step = 1 if way == 0 else -1
        there = line.o + step
        inside = there < line.outer if way == 0 else there >= 0
        device = line.device(lax.rem(there + line.outer, line.outer) * line.inner + line.i)
        return inside, device

    def spread(self, h, index, ways):
        for way in ways:
            inside, device = self.side(way)

            @pl.when(inside)
            def _():
                self.copy(h, index, way, device).start()

        if self.line.inner == 2:
            self.copy(h, index, 2, self.line.mate()).start()

    def start(self, h):
        self.spread(h, self.line.me, (0, 1))

    def other(self):
        line = self.line
        return line.device(lax.rem(line.me + 1, line.count))

    def each_source(self, k, body):
        line = self.line
        for way, source in ((0, line.o - 1 - k), (1, line.o + 1 + k)):
            pl.when(jnp.logical_and(source >= 0, source < line.outer))(
                functools.partial(body, way, source))

    def relay(self, k, h, use):
        def arrived(way, source):
            index = source * self.line.inner + self.line.i
            self.copy(h, index, way, self.other()).wait_recv()
            self.spread(h, index, (way,))
            if use is not None:
                use(index)

        self.each_source(k, arrived)

    def passed(self, k, h, use):
        def arrived(way, source):
            index = source * self.line.inner + 1 - self.line.i
            self.copy(h, index, 2, self.other()).wait_recv()
            if use is not None:
                use(index)

        if isinstance(k, int) and k < 0:
            arrived(2, self.line.o)
        else:
            self.each_source(k, arrived)

    def drain(self, h):
        line = self.line

        def one(source):
            index = source * line.inner + line.i
            for way in (0, 1):
                inside, device = self.side(way)
                went = source <= line.o if way == 0 else source >= line.o

                @pl.when(jnp.logical_and(inside, went))
                def _():
                    self.copy(h, index, way, device).wait_send()

            if line.inner == 2:
                self.copy(h, index, 2, line.mate()).wait_send()

        each(line.outer, one)


class Scatter:
    def __init__(self, line, near, near_in, far, far_in, total, sems):
        self.line, self.total = line, total
        self.near, self.near_in, self.far, self.far_in = near, near_in, far, far_in
        self.near_sent, self.near_landed, self.far_sent, self.far_landed = sems

    def near_copy(self, h, o2):
        return remote(
            self.near.at[h, o2], self.near_in.at[h, o2], self.near_sent.at[h, o2],
            self.near_landed.at[h, o2], self.line.mate(),
        )

    def far_copy(self, h, o2, source):
        return remote(
            self.far.at[h, o2], self.far_in.at[h, source], self.far_sent.at[h, o2],
            self.far_landed.at[h, source], self.line.device(o2 * self.line.inner + self.line.i),
        )

    def start(self, h, partial):
        line = self.line

        def one(k):
            o2 = line.ahead(k)
            if partial is not None:
                self.near[h, o2] = partial(h, o2 * line.inner + 1 - line.i).astype(BF16)
            self.near_copy(h, o2).start()

        if line.inner == 2:
            each(line.outer, one)

    def pair(self, h, o2, partial):
        line = self.line
        value = partial(h, o2 * line.inner + line.i)
        if line.inner == 2:
            self.near_copy(h, o2).wait_recv()
            value = value + self.near_in[h, o2].astype(F32)
        return value

    def middle(self, h, partial, first, last):
        line = self.line

        def one(k):
            o2 = line.ahead(first + k)
            self.far[h, o2] = self.pair(h, o2, partial).astype(BF16)
            self.far_copy(h, o2, line.o).start()

        each(last - first, one)
        if last == line.outer - 1:
            self.total[h] = self.pair(h, line.o, partial)

    def end(self, h):
        line = self.line

        def one(k):
            source = line.behind(k)
            self.far_copy(h, line.ahead(0), source).wait_recv()
            self.total[h] += self.far_in[h, source].astype(F32)

        each(line.outer - 1, one)
        return self.total[h]

    def drain(self, h):
        line = self.line
        if line.inner == 2:
            each(line.outer, lambda k: self.near_copy(h, k).wait_send())
        each(line.outer - 1, lambda k: self.far_copy(h, line.ahead(k), line.o).wait_send())


def kernel(
    rows_n, cols_n, scale,
    coords, features, weight, cotangent, values,
    activated, dfeatures, dweight,
    xg, xg_sent, xg_landed,
    dense, flipped,
    c_near, c_near_in, c_far, c_far_in, c_total, c_ns, c_nl, c_fs, c_fl,
    sg, sg_sent, sg_landed,
    grad,
    e_near, e_near_in, e_far, e_far_in, e_total, e_ns, e_nl, e_fs, e_fl,
    w1, w1_in, w1_sent, w1_landed,
    w2, w2_in, w2_sent, w2_landed,
    wcopy, wide, mixed, stock, turned, fetched, kept,
):
    r, c = lax.axis_index("row"), lax.axis_index("col")
    row = Line("row", rows_n, lambda index: (index, c))
    col = Line("col", cols_n, lambda index: (r, index))
    own, hidden = features.shape
    width = hidden // PARTS
    slots, block = values.shape[0], values.shape[1]

    barrier = pltpu.get_barrier_semaphore()
    each(rows_n - 1, lambda k: pl.semaphore_signal(
        barrier, inc=1, device_id=row.device(lax.rem(r + k + 1, rows_n)), device_id_type=MESH))
    each(cols_n - 1, lambda k: pl.semaphore_signal(
        barrier, inc=1, device_id=col.device(lax.rem(c + k + 1, cols_n)), device_id_type=MESH))
    fetch_values = pltpu.make_async_copy(values, stock.at[pl.ds(0, slots)], fetched.at[0])
    fetch_weight = pltpu.make_async_copy(weight, wide, fetched.at[1])
    fetch_values.start()
    fetch_weight.start()
    for h in range(PARTS):
        xg[h, r] = features[:, h * width:(h + 1) * width].astype(BF16)
    stock[slots] = jnp.zeros((block, block), BF16)
    pl.semaphore_wait(barrier, rows_n + cols_n - 2)

    xs = Gather(row, xg, xg_sent, xg_landed)
    for h in range(PARTS):
        xs.start(h)

    row_blocks, col_blocks = cols_n * own // block, rows_n * own // block
    per = own // block
    short = slots <= 16
    keys = [coords[0, s] * col_blocks + coords[1, s] for s in range(slots)] if short else None

    def place(i):
        for j in range(col_blocks):
            def look(s, found):
                key = keys[s] if short else coords[0, s] * col_blocks + coords[1, s]
                return jnp.where(key == i * col_blocks + j, s, found)

            found = jnp.int32(slots)
            if short:
                for s in range(slots):
                    found = look(s, found)
            else:
                found = lax.fori_loop(0, slots, look, found)
            if per == 1:
                rows, lead = pl.ds(0, block), i
            else:
                rows, lead = pl.ds((i % per) * block, block), i // per
            dense[lead, rows, j * block:(j + 1) * block] = stock[found]
            flipped[lead, j * block:(j + 1) * block, rows] = turned[found]

    def turn(s):
        turned[s] = stock[s].T

    fetch_values.wait()
    each(slots + 1, turn)
    half = row_blocks // 2
    each(half, place)
    each(row.outer - 1, lambda k: xs.relay(0, k))
    each(row_blocks - half, lambda k: place(half + k))
    for h in range(1, PARTS):
        each(row.outer - 1, lambda k: xs.relay(h, k))

    agg = Scatter(col, c_near, c_near_in, c_far, c_far_in, c_total, (c_ns, c_nl, c_fs, c_fl))

    tall = own // PARTS

    def forward(p, side):
        rows = jnp.concatenate(
            [dense[o2 * col.inner + side, p * tall:(p + 1) * tall, :] for o2 in range(col.outer)], axis=0)
        full = jnp.concatenate([xg[h].reshape(rows_n * own, width) for h in range(PARTS)], axis=1)
        return dot(rows, full).reshape(col.outer, tall, hidden)

    def kept_block(p, index):
        return kept[p, index // col.inner]

    for h in range(PARTS):
        if row.inner == 2:
            each(row.outer, lambda k: xs.passed(h, k))
    for p in range(PARTS):
        if col.inner == 2:
            c_near[p] = forward(p, 1 - col.i).astype(BF16)
        agg.start(p, None)
    for p in range(PARTS):
        kept[p] = forward(p, col.i)
    fetch_weight.wait()
    wcopy[...] = wide[...].astype(BF16)

    slopes = Chain(col, sg, sg_sent, sg_landed)

    def own_slope(p):
        span = slice(p * tall, (p + 1) * tall)
        part = agg.end(p).astype(BF16)
        total = dot(part, wcopy[...])
        sigma = jax.nn.sigmoid(total)
        slope = cotangent[span, :].astype(F32) * (sigma * (1.0 + total * (1.0 - sigma)))
        sg[p, c] = slope.astype(BF16)
        slopes.start(p)
        mixed[span, :] = part
        activated[span, :] = total * sigma

    hops = col.outer - 1
    for p in range(PARTS):
        early = (hops + 1) // 2 if p else hops
        agg.middle(p, kept_block, 0, early)
        if p:
            own_slope(p - 1)
            agg.middle(p, kept_block, early, hops)
            each(min(hops, 1), lambda k: slopes.relay(k, p - 1, None))
    own_slope(PARTS - 1)

    def both(index):
        return jnp.concatenate([sg[p, index] for p in range(PARTS)], axis=0)

    share = hidden // rows_n
    w1[...] = dot(mixed[...], both(c), 0, 0).reshape(rows_n, share, hidden).astype(BF16)

    def w1_copy(k):
        to = lax.rem(r + k + 1, rows_n)
        return remote(w1.at[to], w1_in.at[r], w1_sent.at[to], w1_landed.at[r], row.device(to))

    each(rows_n - 1, lambda k: w1_copy(k).start())

    def add(index, h):
        pair = [(index // col.inner) * col.inner + i for i in range(col.inner)]
        span = slice(h * width, (h + 1) * width)
        left = jnp.concatenate([flipped[i] for i in pair], axis=1)
        right = jnp.concatenate([sg[p, i, :, span] for i in pair for p in range(PARTS)], axis=0)
        grad[h] += dot(left, right)

    def add_all(index):
        for h in range(PARTS):
            add(index, h)

    for h in range(PARTS):
        grad[h] = jnp.zeros(grad.shape[1:], F32)
    alone = add_all if col.inner == 1 else None
    for p in range(PARTS):
        seen = min(hops, 1) if p < PARTS - 1 else 0
        each(hops - seen, lambda k: slopes.relay(seen + k, p, alone if p == PARTS - 1 else None))
    if col.inner == 1:
        add_all(c)

    nodes = Scatter(row, e_near, e_near_in, e_far, e_far_in, e_total, (e_ns, e_nl, e_fs, e_fl))

    def term(h, index):
        return grad[h, pl.ds(pl.multiple_of(index * own, own), own), :]

    def w1_wait(k):
        source = lax.rem(r + rows_n - k - 1, rows_n)
        remote(w1.at[source], w1_in.at[source], w1_sent.at[source], w1_landed.at[source],
               row.device(source)).wait_recv()
        return source

    def w2_copy(k):
        to = lax.rem(c + k + 1, cols_n)
        return remote(w2.at[to], w2_in.at[c], w2_sent.at[to], w2_landed.at[c], col.device(to))

    def w2_wait(k):
        source = lax.rem(c + cols_n - k - 1, cols_n)
        remote(w2.at[source], w2_in.at[source], w2_sent.at[source], w2_landed.at[source],
               col.device(source)).wait_recv()

    each(rows_n - 1, w1_wait)
    w1_in[r] = w1[r]
    weight_sum = jnp.sum(w1_in[...].astype(F32), axis=0)
    w2[...] = weight_sum.T.reshape(cols_n, hidden // cols_n, share).astype(w2.dtype)
    each(cols_n - 1, lambda k: w2_copy(k).start())
    w2_in[c] = w2[c]

    for p in range(PARTS):
        if col.inner == 2:
            use = add_all if p == PARTS - 1 else None
            slopes.passed(-1, p, use)
            each(hops, lambda k: slopes.passed(k, p, use))
    for h in range(PARTS):
        nodes.start(h, term)
    for h in range(PARTS):
        nodes.middle(h, term, 0, row.outer - 1)

    out = None
    for h in range(PARTS):
        grad16 = nodes.end(h).astype(BF16)
        piece = dot(grad16, wcopy[:, h * width:(h + 1) * width], 1, 1)
        out = piece if out is None else out + piece
    dfeatures[...] = out

    each(cols_n - 1, w2_wait)
    dweight[...] = jnp.sum(w2_in[...].astype(F32), axis=0) * scale

    for h in range(PARTS):
        xs.drain(h)
        agg.drain(h)
        slopes.drain(h)
        nodes.drain(h)
    each(rows_n - 1, lambda k: w1_copy(k).wait_send())
    each(cols_n - 1, lambda k: w2_copy(k).wait_send())


def hand_over(a, b, c, a_out, b_out, c_out, a_held, b_held, c_held, sems):
    rows = ((a, a_held, a_out), (b, b_held, b_out), (c, c_held, c_out))
    ins = [pltpu.make_async_copy(src, held, sems.at[0, k]) for k, (src, held, _) in enumerate(rows)]
    outs = [pltpu.make_async_copy(held, dst, sems.at[1, k]) for k, (_, held, dst) in enumerate(rows)]
    for copy in ins:
        copy.start()
    for copy, after in zip(ins, outs):
        copy.wait()
        after.start()
    for copy in outs:
        copy.wait()


def on_device(rows_n, cols_n, features, weight, cotangent, block_values, block_coords):
    values, coords = block_values[0, 0], block_coords[0, 0]
    own, hidden = features.shape
    width = hidden // PARTS
    row_in, col_in = inner_size(rows_n), inner_size(cols_n)
    row_out, col_out = rows_n // row_in, cols_n // col_in
    scale = 1.0 / (own * rows_n * cols_n) ** 0.5
    share_r, share_c = hidden // rows_n, hidden // cols_n
    dma = pltpu.SemaphoreType.DMA

    def gather_scratch(count, outer):
        return [
            pltpu.VMEM((PARTS, count, own, width), BF16),
            dma((PARTS, 2 * outer)),
            dma((PARTS, count)),
        ]

    def scatter_scratch(outer, piece):
        return (
            [pltpu.VMEM((PARTS, outer) + piece, BF16)] * 4
            + [pltpu.VMEM((PARTS,) + piece, F32)]
            + [dma((PARTS, outer))] * 4
        )

    scratch = (
        gather_scratch(rows_n, row_out)
        + [
            pltpu.VMEM((cols_n, own, rows_n * own), BF16),
            pltpu.VMEM((cols_n, rows_n * own, own), BF16),
        ]
        + scatter_scratch(col_out, (own // PARTS, hidden))
        + [
            pltpu.VMEM((PARTS, cols_n, own // PARTS, hidden), BF16),
            dma((PARTS, col_out, 3)),
            dma((PARTS, cols_n)),
        ]
        + [pltpu.VMEM((PARTS, rows_n * own, width), F32)]
        + scatter_scratch(row_out, (own, width))
        + [pltpu.VMEM((rows_n, share_r, hidden), BF16)] * 2
        + [dma((rows_n,))] * 2
        + [pltpu.VMEM((cols_n, share_c, share_r), BF16)] * 2
        + [dma((cols_n,))] * 2
        + [
            pltpu.VMEM((hidden, hidden), BF16),
            pltpu.VMEM((hidden, hidden), F32),
            pltpu.VMEM((own, hidden), BF16),
            pltpu.VMEM((values.shape[0] + 1,) + values.shape[1:], BF16),
            pltpu.VMEM((values.shape[0] + 1,) + values.shape[1:], BF16),
            dma((2,)),
            pltpu.VMEM((PARTS, col_out, own // PARTS, hidden), F32),
        ]
    )
    vmem = pl.BlockSpec(memory_space=pltpu.VMEM)
    anywhere = pl.BlockSpec(memory_space=pl.ANY)
    results = pl.pallas_call(
        functools.partial(kernel, rows_n, cols_n, scale),
        out_shape=(
            jax.ShapeDtypeStruct((own, hidden), F32),
            jax.ShapeDtypeStruct((own, hidden), F32),
            jax.ShapeDtypeStruct((share_c, share_r), F32),
        ),
        in_specs=[pl.BlockSpec(memory_space=pltpu.SMEM), vmem, anywhere, vmem, anywhere],
        out_specs=(vmem, vmem, vmem),
        scratch_shapes=scratch,
        compiler_params=pltpu.CompilerParams(
            collective_id=0, has_side_effects=True, vmem_limit_bytes=56 * 1024 * 1024
        ),
    )(coords, features, weight, cotangent, values)
    ours, theirs, flat = pl.pallas_call(
        hand_over,
        out_shape=tuple(jax.ShapeDtypeStruct(a.shape, a.dtype) for a in results),
        in_specs=[pl.BlockSpec(memory_space=pltpu.HBM)] * 3,
        out_specs=(pl.BlockSpec(memory_space=pltpu.HBM),) * 3,
        scratch_shapes=[pltpu.VMEM(a.shape, a.dtype) for a in results] + [dma((2, 3))],
        compiler_params=pltpu.CompilerParams(vmem_limit_bytes=60 * 1024 * 1024),
    )(*results)
    return ours, theirs, flat.T


def solution(mesh):
    placed = (
        P(("col", "row"), None),
        P(),
        P(("row", "col"), None),
        P("row", "col", None, None, None),
        P("row", "col", None, None),
    )
    return jax.shard_map(
        functools.partial(on_device, mesh.shape["row"], mesh.shape["col"]),
        mesh=mesh,
        in_specs=placed,
        out_specs=(P(("row", "col"), None), P(("col", "row"), None), P("row", "col")),
        check_vma=False,
    )
```

```python
import functools

import jax
import jax.numpy as jnp
from jax import lax
from jax.experimental import pallas as pl
from jax.experimental.pallas import tpu as pltpu
from jax.sharding import PartitionSpec as P

MESH = pl.DeviceIdType.MESH
PARTS = 2
F32, BF16 = jnp.float32, jnp.bfloat16


def each(count, body):
    if count <= 8:
        for k in range(count):
            body(k)
    else:
        lax.fori_loop(0, count, lambda k, carry: (body(k), carry)[1], 0)


def inner_size(count):
    return 2 if count % 2 == 0 else 1


def dot(a, b, left=1, right=0):
    return lax.dot_general(a, b, (((left,), (right,)), ((), ())), preferred_element_type=F32)


def remote(src, dst, sent, landed, device):
    return pltpu.make_async_remote_copy(
        src_ref=src, dst_ref=dst, send_sem=sent, recv_sem=landed, device_id=device, device_id_type=MESH
    )


class Line:
    def __init__(self, name, count, device):
        self.count, self.device = count, device
        self.inner = inner_size(count)
        self.outer = count // self.inner
        self.me = lax.axis_index(name)
        self.o = self.me // self.inner
        self.i = self.me % self.inner

    def ahead(self, k):
        return lax.rem(self.o + k + 1, self.outer)

    def behind(self, k):
        return lax.rem(self.o + self.outer - k - 1, self.outer)

    def mate(self):
        return self.device(self.o * self.inner + 1 - self.i)


class Gather:
    def __init__(self, line, buf, sent, landed):
        self.line, self.buf, self.sent, self.landed = line, buf, sent, landed

    def copy(self, h, index, slot, device):
        piece = self.buf.at[h, index]
        return remote(piece, piece, self.sent.at[h, slot], self.landed.at[h, index], device)

    def start(self, h):
        line = self.line

        def far(k):
            self.copy(h, line.me, k, line.device(line.ahead(k) * line.inner + line.i)).start()

        if line.inner == 2:
            self.copy(h, line.me, line.outer - 1, line.mate()).start()
        each(line.outer - 1, far)

    def any_peer(self):
        line = self.line
        return line.device(lax.rem(line.me + 1, line.count))

    def relay(self, h, k):
        line = self.line
        index = line.behind(k) * line.inner + line.i
        self.copy(h, index, k, self.any_peer()).wait_recv()
        if line.inner == 2:
            self.copy(h, index, line.outer + k, line.mate()).start()
        return index

    def passed(self, h, k):
        line = self.line
        index = line.behind(k - 1) * line.inner + 1 - line.i
        self.copy(h, index, 0, self.any_peer()).wait_recv()
        return index

    def drain(self, h):
        line = self.line
        slots = 2 * line.outer - 1 if line.inner == 2 else line.outer - 1
        each(slots, lambda k: self.copy(h, line.me, k, self.any_peer()).wait_send())


class Chain:
    def __init__(self, line, buf, sent, landed):
        self.line, self.buf, self.sent, self.landed = line, buf, sent, landed

    def copy(self, h, index, way, device):
        piece = self.buf.at[h, index]
        return remote(
            piece, piece, self.sent.at[h, index // self.line.inner, way], self.landed.at[h, index], device
        )

    def side(self, way):
        line = self.line
        step = 1 if way == 0 else -1
        there = line.o + step
        inside = there < line.outer if way == 0 else there >= 0
        device = line.device(lax.rem(there + line.outer, line.outer) * line.inner + line.i)
        return inside, device

    def spread(self, h, index, ways):
        for way in ways:
            inside, device = self.side(way)

            @pl.when(inside)
            def _():
                self.copy(h, index, way, device).start()

        if self.line.inner == 2:
            self.copy(h, index, 2, self.line.mate()).start()

    def start(self, h):
        self.spread(h, self.line.me, (0, 1))

    def other(self):
        line = self.line
        return line.device(lax.rem(line.me + 1, line.count))

    def each_source(self, k, body):
        line = self.line
        for way, source in ((0, line.o - 1 - k), (1, line.o + 1 + k)):
            pl.when(jnp.logical_and(source >= 0, source < line.outer))(
                functools.partial(body, way, source))

    def relay(self, k, h, use):
        def arrived(way, source):
            index = source * self.line.inner + self.line.i
            self.copy(h, index, way, self.other()).wait_recv()
            self.spread(h, index, (way,))
            if use is not None:
                use(index)

        self.each_source(k, arrived)

    def passed(self, k, h, use):
        def arrived(way, source):
            index = source * self.line.inner + 1 - self.line.i
            self.copy(h, index, 2, self.other()).wait_recv()
            if use is not None:
                use(index)

        if isinstance(k, int) and k < 0:
            arrived(2, self.line.o)
        else:
            self.each_source(k, arrived)

    def drain(self, h):
        line = self.line

        def one(source):
            index = source * line.inner + line.i
            for way in (0, 1):
                inside, device = self.side(way)
                went = source <= line.o if way == 0 else source >= line.o

                @pl.when(jnp.logical_and(inside, went))
                def _():
                    self.copy(h, index, way, device).wait_send()

            if line.inner == 2:
                self.copy(h, index, 2, line.mate()).wait_send()

        each(line.outer, one)


class Scatter:
    def __init__(self, line, near, near_in, far, far_in, total, sems):
        self.line, self.total = line, total
        self.near, self.near_in, self.far, self.far_in = near, near_in, far, far_in
        self.near_sent, self.near_landed, self.far_sent, self.far_landed = sems

    def near_copy(self, h, o2):
        return remote(
            self.near.at[h, o2], self.near_in.at[h, o2], self.near_sent.at[h, o2],
            self.near_landed.at[h, o2], self.line.mate(),
        )

    def far_copy(self, h, o2, source):
        return remote(
            self.far.at[h, o2], self.far_in.at[h, source], self.far_sent.at[h, o2],
            self.far_landed.at[h, source], self.line.device(o2 * self.line.inner + self.line.i),
        )

    def start(self, h, partial):
        line = self.line

        def one(k):
            o2 = line.ahead(k)
            if partial is not None:
                self.near[h, o2] = partial(h, o2 * line.inner + 1 - line.i).astype(BF16)
            self.near_copy(h, o2).start()

        if line.inner == 2:
            each(line.outer, one)

    def pair(self, h, o2, partial):
        line = self.line
        value = partial(h, o2 * line.inner + line.i)
        if line.inner == 2:
            self.near_copy(h, o2).wait_recv()
            value = value + self.near_in[h, o2].astype(F32)
        return value

    def middle(self, h, partial, first, last):
        line = self.line

        def one(k):
            o2 = line.ahead(first + k)
            self.far[h, o2] = self.pair(h, o2, partial).astype(BF16)
            self.far_copy(h, o2, line.o).start()

        each(last - first, one)
        if last == line.outer - 1:
            self.total[h] = self.pair(h, line.o, partial)

    def end(self, h):
        line = self.line

        def one(k):
            source = line.behind(k)
            self.far_copy(h, line.ahead(0), source).wait_recv()
            self.total[h] += self.far_in[h, source].astype(F32)

        each(line.outer - 1, one)
        return self.total[h]

    def drain(self, h):
        line = self.line
        if line.inner == 2:
            each(line.outer, lambda k: self.near_copy(h, k).wait_send())
        each(line.outer - 1, lambda k: self.far_copy(h, line.ahead(k), line.o).wait_send())


def kernel(
    rows_n, cols_n, scale,
    coords, features_in, weight, cotangent_in, values,
    activated_out, dfeatures_out, dweight_out,
    features, cotangent, activated, dfeatures, dweight, moved,
    xg, xg_sent, xg_landed,
    dense, flipped,
    c_near, c_near_in, c_far, c_far_in, c_total, c_ns, c_nl, c_fs, c_fl,
    sg, sg_sent, sg_landed,
    grad,
    e_near, e_near_in, e_far, e_far_in, e_total, e_ns, e_nl, e_fs, e_fl,
    w1, w1_in, w1_sent, w1_landed,
    w2, w2_in, w2_sent, w2_landed,
    wcopy, wide, mixed, stock, turned, fetched, kept,
):
    r, c = lax.axis_index("row"), lax.axis_index("col")
    row = Line("row", rows_n, lambda index: (index, c))
    col = Line("col", cols_n, lambda index: (r, index))
    own, hidden = features.shape
    width = hidden // PARTS
    slots, block = values.shape[0], values.shape[1]

    barrier = pltpu.get_barrier_semaphore()
    each(rows_n - 1, lambda k: pl.semaphore_signal(
        barrier, inc=1, device_id=row.device(lax.rem(r + k + 1, rows_n)), device_id_type=MESH))
    each(cols_n - 1, lambda k: pl.semaphore_signal(
        barrier, inc=1, device_id=col.device(lax.rem(c + k + 1, cols_n)), device_id_type=MESH))
    fetch_values = pltpu.make_async_copy(values, stock.at[pl.ds(0, slots)], fetched.at[0])
    fetch_weight = pltpu.make_async_copy(weight, wide, fetched.at[1])
    fetch_features = pltpu.make_async_copy(features_in, features, moved.at[0])
    fetch_cotangent = pltpu.make_async_copy(cotangent_in, cotangent, moved.at[1])
    fetch_features.start()
    fetch_values.start()
    fetch_cotangent.start()
    fetch_weight.start()
    fetch_features.wait()
    for h in range(PARTS):
        xg[h, r] = features[:, h * width:(h + 1) * width].astype(BF16)
    stock[slots] = jnp.zeros((block, block), BF16)
    pl.semaphore_wait(barrier, rows_n + cols_n - 2)

    xs = Gather(row, xg, xg_sent, xg_landed)
    for h in range(PARTS):
        xs.start(h)

    row_blocks, col_blocks = cols_n * own // block, rows_n * own // block
    per = own // block
    short = slots <= 16
    keys = [coords[0, s] * col_blocks + coords[1, s] for s in range(slots)] if short else None

    def place(i):
        for j in range(col_blocks):
            def look(s, found):
                key = keys[s] if short else coords[0, s] * col_blocks + coords[1, s]
                return jnp.where(key == i * col_blocks + j, s, found)

            found = jnp.int32(slots)
            if short:
                for s in range(slots):
                    found = look(s, found)
            else:
                found = lax.fori_loop(0, slots, look, found)
            if per == 1:
                rows, lead = pl.ds(0, block), i
            else:
                rows, lead = pl.ds((i % per) * block, block), i // per
            dense[lead, rows, j * block:(j + 1) * block] = stock[found]
            flipped[lead, j * block:(j + 1) * block, rows] = turned[found]

    def turn(s):
        turned[s] = stock[s].T

    fetch_values.wait()
    each(slots + 1, turn)
    half = row_blocks // 2
    each(half, place)
    each(row.outer - 1, lambda k: xs.relay(0, k))
    each(row_blocks - half, lambda k: place(half + k))
    for h in range(1, PARTS):
        each(row.outer - 1, lambda k: xs.relay(h, k))

    agg = Scatter(col, c_near, c_near_in, c_far, c_far_in, c_total, (c_ns, c_nl, c_fs, c_fl))

    tall = own // PARTS

    def forward(p, side):
        rows = jnp.concatenate(
            [dense[o2 * col.inner + side, p * tall:(p + 1) * tall, :] for o2 in range(col.outer)], axis=0)
        full = jnp.concatenate([xg[h].reshape(rows_n * own, width) for h in range(PARTS)], axis=1)
        return dot(rows, full).reshape(col.outer, tall, hidden)

    def kept_block(p, index):
        return kept[p, index // col.inner]

    for h in range(PARTS):
        if row.inner == 2:
            each(row.outer, lambda k: xs.passed(h, k))
    for p in range(PARTS):
        if col.inner == 2:
            c_near[p] = forward(p, 1 - col.i).astype(BF16)
        agg.start(p, None)
    for p in range(PARTS):
        kept[p] = forward(p, col.i)
    fetch_weight.wait()
    fetch_cotangent.wait()
    wcopy[...] = wide[...].astype(BF16)

    slopes = Chain(col, sg, sg_sent, sg_landed)

    def own_slope(p):
        span = slice(p * tall, (p + 1) * tall)
        part = agg.end(p).astype(BF16)
        total = dot(part, wcopy[...])
        sigma = jax.nn.sigmoid(total)
        slope = cotangent[span, :].astype(F32) * (sigma * (1.0 + total * (1.0 - sigma)))
        sg[p, c] = slope.astype(BF16)
        slopes.start(p)
        mixed[span, :] = part
        activated[span, :] = total * sigma

    hops = col.outer - 1
    for p in range(PARTS):
        early = (hops + 1) // 2 if p else hops
        agg.middle(p, kept_block, 0, early)
        if p:
            own_slope(p - 1)
            agg.middle(p, kept_block, early, hops)
            each(min(hops, 1), lambda k: slopes.relay(k, p - 1, None))
    own_slope(PARTS - 1)
    give_activated = pltpu.make_async_copy(activated, activated_out, moved.at[2])
    give_dfeatures = pltpu.make_async_copy(dfeatures, dfeatures_out, moved.at[3])
    give_dweight = pltpu.make_async_copy(dweight, dweight_out, moved.at[4])
    give_activated.start()

    def both(index):
        return jnp.concatenate([sg[p, index] for p in range(PARTS)], axis=0)

    share = hidden // rows_n
    w1[...] = dot(mixed[...], both(c), 0, 0).reshape(rows_n, share, hidden).astype(BF16)

    def w1_copy(k):
        to = lax.rem(r + k + 1, rows_n)
        return remote(w1.at[to], w1_in.at[r], w1_sent.at[to], w1_landed.at[r], row.device(to))

    each(rows_n - 1, lambda k: w1_copy(k).start())

    def add(index, h):
        pair = [(index // col.inner) * col.inner + i for i in range(col.inner)]
        span = slice(h * width, (h + 1) * width)
        left = jnp.concatenate([flipped[i] for i in pair], axis=1)
        right = jnp.concatenate([sg[p, i, :, span] for i in pair for p in range(PARTS)], axis=0)
        grad[h] += dot(left, right)

    def add_first(index):
        add(index, 0)

    for h in range(PARTS):
        grad[h] = jnp.zeros(grad.shape[1:], F32)
    alone = add_first if col.inner == 1 else None
    for p in range(PARTS):
        seen = min(hops, 1) if p < PARTS - 1 else 0
        each(hops - seen, lambda k: slopes.relay(seen + k, p, alone if p == PARTS - 1 else None))
    if col.inner == 1:
        add_first(c)

    nodes = Scatter(row, e_near, e_near_in, e_far, e_far_in, e_total, (e_ns, e_nl, e_fs, e_fl))

    def term(h, index):
        return grad[h, pl.ds(pl.multiple_of(index * own, own), own), :]

    def w1_wait(k):
        source = lax.rem(r + rows_n - k - 1, rows_n)
        remote(w1.at[source], w1_in.at[source], w1_sent.at[source], w1_landed.at[source],
               row.device(source)).wait_recv()
        return source

    def w2_copy(k):
        to = lax.rem(c + k + 1, cols_n)
        return remote(w2.at[to], w2_in.at[c], w2_sent.at[to], w2_landed.at[c], col.device(to))

    def w2_wait(k):
        source = lax.rem(c + cols_n - k - 1, cols_n)
        remote(w2.at[source], w2_in.at[source], w2_sent.at[source], w2_landed.at[source],
               col.device(source)).wait_recv()

    each(rows_n - 1, w1_wait)
    w1_in[r] = w1[r]
    weight_sum = jnp.sum(w1_in[...].astype(F32), axis=0)
    w2[...] = weight_sum.T.reshape(cols_n, hidden // cols_n, share).astype(w2.dtype)
    each(cols_n - 1, lambda k: w2_copy(k).start())
    w2_in[c] = w2[c]

    for p in range(PARTS):
        if col.inner == 2:
            use = add_first if p == PARTS - 1 else None
            slopes.passed(-1, p, use)
            each(hops, lambda k: slopes.passed(k, p, use))
    for h in range(PARTS):
        if h:
            each(col.outer, lambda k: add(k * col.inner, h))
        nodes.start(h, term)
    for h in range(PARTS):
        nodes.middle(h, term, 0, row.outer - 1)

    each(cols_n - 1, w2_wait)
    dweight[...] = jnp.sum(w2_in[...].astype(F32), axis=0) * scale
    give_dweight.start()

    out = None
    for h in range(PARTS):
        grad16 = nodes.end(h).astype(BF16)
        piece = dot(grad16, wcopy[:, h * width:(h + 1) * width], 1, 1)
        out = piece if out is None else out + piece
    dfeatures[...] = out
    give_dfeatures.start()

    for h in range(PARTS):
        xs.drain(h)
        agg.drain(h)
        slopes.drain(h)
        nodes.drain(h)
    each(rows_n - 1, lambda k: w1_copy(k).wait_send())
    each(cols_n - 1, lambda k: w2_copy(k).wait_send())
    for give in (give_activated, give_dweight, give_dfeatures):
        give.wait()


def hand_over(a, b, c, a_out, b_out, c_out, a_held, b_held, c_held, sems):
    rows = ((a, a_held, a_out), (b, b_held, b_out), (c, c_held, c_out))
    ins = [pltpu.make_async_copy(src, held, sems.at[0, k]) for k, (src, held, _) in enumerate(rows)]
    outs = [pltpu.make_async_copy(held, dst, sems.at[1, k]) for k, (_, held, dst) in enumerate(rows)]
    for copy in ins:
        copy.start()
    for copy, after in zip(ins, outs):
        copy.wait()
        after.start()
    for copy in outs:
        copy.wait()


def on_device(rows_n, cols_n, features, weight, cotangent, block_values, block_coords):
    values, coords = block_values[0, 0], block_coords[0, 0]
    own, hidden = features.shape
    width = hidden // PARTS
    row_in, col_in = inner_size(rows_n), inner_size(cols_n)
    row_out, col_out = rows_n // row_in, cols_n // col_in
    scale = 1.0 / (own * rows_n * cols_n) ** 0.5
    share_r, share_c = hidden // rows_n, hidden // cols_n
    dma = pltpu.SemaphoreType.DMA

    def gather_scratch(count, outer):
        return [
            pltpu.VMEM((PARTS, count, own, width), BF16),
            dma((PARTS, 2 * outer)),
            dma((PARTS, count)),
        ]

    def scatter_scratch(outer, piece):
        return (
            [pltpu.VMEM((PARTS, outer) + piece, BF16)] * 4
            + [pltpu.VMEM((PARTS,) + piece, F32)]
            + [dma((PARTS, outer))] * 4
        )

    scratch = (
        [
            pltpu.VMEM((own, hidden), F32),
            pltpu.VMEM((own, hidden), BF16),
            pltpu.VMEM((own, hidden), F32),
            pltpu.VMEM((own, hidden), F32),
            pltpu.VMEM((share_c, share_r), F32),
            dma((5,)),
        ]
        + gather_scratch(rows_n, row_out)
        + [
            pltpu.VMEM((cols_n, own, rows_n * own), BF16),
            pltpu.VMEM((cols_n, rows_n * own, own), BF16),
        ]
        + scatter_scratch(col_out, (own // PARTS, hidden))
        + [
            pltpu.VMEM((PARTS, cols_n, own // PARTS, hidden), BF16),
            dma((PARTS, col_out, 3)),
            dma((PARTS, cols_n)),
        ]
        + [pltpu.VMEM((PARTS, rows_n * own, width), F32)]
        + scatter_scratch(row_out, (own, width))
        + [pltpu.VMEM((rows_n, share_r, hidden), BF16)] * 2
        + [dma((rows_n,))] * 2
        + [pltpu.VMEM((cols_n, share_c, share_r), BF16)] * 2
        + [dma((cols_n,))] * 2
        + [
            pltpu.VMEM((hidden, hidden), BF16),
            pltpu.VMEM((hidden, hidden), F32),
            pltpu.VMEM((own, hidden), BF16),
            pltpu.VMEM((values.shape[0] + 1,) + values.shape[1:], BF16),
            pltpu.VMEM((values.shape[0] + 1,) + values.shape[1:], BF16),
            dma((2,)),
            pltpu.VMEM((PARTS, col_out, own // PARTS, hidden), F32),
        ]
    )
    anywhere = pl.BlockSpec(memory_space=pl.ANY)
    results = pl.pallas_call(
        functools.partial(kernel, rows_n, cols_n, scale),
        out_shape=(
            jax.ShapeDtypeStruct((own, hidden), F32),
            jax.ShapeDtypeStruct((own, hidden), F32),
            jax.ShapeDtypeStruct((share_c, share_r), F32),
        ),
        in_specs=[pl.BlockSpec(memory_space=pltpu.SMEM)] + [anywhere] * 4,
        out_specs=(anywhere,) * 3,
        scratch_shapes=scratch,
        compiler_params=pltpu.CompilerParams(
            collective_id=0, has_side_effects=True, vmem_limit_bytes=56 * 1024 * 1024
        ),
    )(coords, features, weight, cotangent, values)
    ours, theirs, flat = pl.pallas_call(
        hand_over,
        out_shape=tuple(jax.ShapeDtypeStruct(a.shape, a.dtype) for a in results),
        in_specs=[pl.BlockSpec(memory_space=pltpu.HBM)] * 3,
        out_specs=(pl.BlockSpec(memory_space=pltpu.HBM),) * 3,
        scratch_shapes=[pltpu.VMEM(a.shape, a.dtype) for a in results] + [dma((2, 3))],
        compiler_params=pltpu.CompilerParams(vmem_limit_bytes=60 * 1024 * 1024),
    )(*results)
    return ours, theirs, flat.T


def solution(mesh):
    placed = (
        P(("col", "row"), None),
        P(),
        P(("row", "col"), None),
        P("row", "col", None, None, None),
        P("row", "col", None, None),
    )
    return jax.shard_map(
        functools.partial(on_device, mesh.shape["row"], mesh.shape["col"]),
        mesh=mesh,
        in_specs=placed,
        out_specs=(P(("row", "col"), None), P(("col", "row"), None), P("row", "col")),
        check_vma=False,
    )
```

```python
import functools

import jax
import jax.numpy as jnp
from jax import lax
from jax.experimental import pallas as pl
from jax.experimental.pallas import tpu as pltpu
from jax.sharding import PartitionSpec as P

MESH = pl.DeviceIdType.MESH
PARTS = 2
F32, BF16 = jnp.float32, jnp.bfloat16


def each(count, body):
    if count <= 8:
        for k in range(count):
            body(k)
    else:
        lax.fori_loop(0, count, lambda k, carry: (body(k), carry)[1], 0)


def inner_size(count):
    return 2 if count % 2 == 0 else 1


def dot(a, b, left=1, right=0):
    return lax.dot_general(a, b, (((left,), (right,)), ((), ())), preferred_element_type=F32)


def remote(src, dst, sent, landed, device):
    return pltpu.make_async_remote_copy(
        src_ref=src, dst_ref=dst, send_sem=sent, recv_sem=landed, device_id=device, device_id_type=MESH
    )


class Line:
    def __init__(self, name, count, device):
        self.count, self.device = count, device
        self.inner = inner_size(count)
        self.outer = count // self.inner
        self.me = lax.axis_index(name)
        self.o = self.me // self.inner
        self.i = self.me % self.inner

    def ahead(self, k):
        return lax.rem(self.o + k + 1, self.outer)

    def behind(self, k):
        return lax.rem(self.o + self.outer - k - 1, self.outer)

    def mate(self):
        return self.device(self.o * self.inner + 1 - self.i)


class Gather:
    def __init__(self, line, buf, sent, landed):
        self.line, self.buf, self.sent, self.landed = line, buf, sent, landed

    def copy(self, h, index, slot, device):
        piece = self.buf.at[h, index]
        return remote(piece, piece, self.sent.at[h, slot], self.landed.at[h, index], device)

    def start(self, h):
        line = self.line

        def far(k):
            self.copy(h, line.me, k, line.device(line.ahead(k) * line.inner + line.i)).start()

        if line.inner == 2:
            self.copy(h, line.me, line.outer - 1, line.mate()).start()
        each(line.outer - 1, far)

    def any_peer(self):
        line = self.line
        return line.device(lax.rem(line.me + 1, line.count))

    def relay(self, h, k):
        line = self.line
        index = line.behind(k) * line.inner + line.i
        self.copy(h, index, k, self.any_peer()).wait_recv()
        if line.inner == 2:
            self.copy(h, index, line.outer + k, line.mate()).start()
        return index

    def passed(self, h, k):
        line = self.line
        index = line.behind(k - 1) * line.inner + 1 - line.i
        self.copy(h, index, 0, self.any_peer()).wait_recv()
        return index

    def drain(self, h):
        line = self.line
        slots = 2 * line.outer - 1 if line.inner == 2 else line.outer - 1
        each(slots, lambda k: self.copy(h, line.me, k, self.any_peer()).wait_send())


class Chain:
    def __init__(self, line, buf, sent, landed):
        self.line, self.buf, self.sent, self.landed = line, buf, sent, landed

    def copy(self, h, index, way, device):
        piece = self.buf.at[h, index]
        return remote(
            piece, piece, self.sent.at[h, index // self.line.inner, way], self.landed.at[h, index], device
        )

    def side(self, way):
        line = self.line
        step = 1 if way == 0 else -1
        there = line.o + step
        inside = there < line.outer if way == 0 else there >= 0
        device = line.device(lax.rem(there + line.outer, line.outer) * line.inner + line.i)
        return inside, device

    def spread(self, h, index, ways):
        for way in ways:
            inside, device = self.side(way)

            @pl.when(inside)
            def _():
                self.copy(h, index, way, device).start()

        if self.line.inner == 2:
            self.copy(h, index, 2, self.line.mate()).start()

    def start(self, h):
        self.spread(h, self.line.me, (0, 1))

    def other(self):
        line = self.line
        return line.device(lax.rem(line.me + 1, line.count))

    def each_source(self, k, body):
        line = self.line
        for way, source in ((0, line.o - 1 - k), (1, line.o + 1 + k)):
            pl.when(jnp.logical_and(source >= 0, source < line.outer))(
                functools.partial(body, way, source))

    def relay(self, k, h, use):
        def arrived(way, source):
            index = source * self.line.inner + self.line.i
            self.copy(h, index, way, self.other()).wait_recv()
            self.spread(h, index, (way,))
            if use is not None:
                use(index)

        self.each_source(k, arrived)

    def passed(self, k, h, use):
        def arrived(way, source):
            index = source * self.line.inner + 1 - self.line.i
            self.copy(h, index, 2, self.other()).wait_recv()
            if use is not None:
                use(index)

        if isinstance(k, int) and k < 0:
            arrived(2, self.line.o)
        else:
            self.each_source(k, arrived)

    def drain(self, h):
        line = self.line

        def one(source):
            index = source * line.inner + line.i
            for way in (0, 1):
                inside, device = self.side(way)
                went = source <= line.o if way == 0 else source >= line.o

                @pl.when(jnp.logical_and(inside, went))
                def _():
                    self.copy(h, index, way, device).wait_send()

            if line.inner == 2:
                self.copy(h, index, 2, line.mate()).wait_send()

        each(line.outer, one)


class Scatter:
    def __init__(self, line, near, near_in, far, far_in, total, sems, cuts):
        self.cuts = cuts
        self.line, self.total = line, total
        self.near, self.near_in, self.far, self.far_in = near, near_in, far, far_in
        self.near_sent, self.near_landed, self.far_sent, self.far_landed = sems

    def near_copies(self, h, o2):
        cuts = self.cuts[h]
        width = self.near.shape[-1] // cuts
        for cut in range(cuts):
            span = pl.ds(cut * width, width)
            yield remote(
                self.near.at[h, o2, :, span], self.near_in.at[h, o2, :, span],
                self.near_sent.at[cut, h, o2], self.near_landed.at[cut, h, o2], self.line.mate(),
            )

    def far_copy(self, h, o2, source):
        return remote(
            self.far.at[h, o2], self.far_in.at[h, source], self.far_sent.at[h, o2],
            self.far_landed.at[h, source], self.line.device(o2 * self.line.inner + self.line.i),
        )

    def start(self, h, partial, cut=None):
        line = self.line

        def one(k):
            o2 = line.ahead(k)
            if partial is not None:
                self.near[h, o2] = partial(h, o2 * line.inner + 1 - line.i).astype(BF16)
            for number, copy in enumerate(self.near_copies(h, o2)):
                if cut is None or cut == number:
                    copy.start()

        if line.inner == 2:
            each(line.outer, one)

    def pair(self, h, o2, partial):
        line = self.line
        value = partial(h, o2 * line.inner + line.i)
        if line.inner == 2:
            for copy in self.near_copies(h, o2):
                copy.wait_recv()
            value = value + self.near_in[h, o2].astype(F32)
        return value

    def middle(self, h, partial, first, last):
        line = self.line

        def one(k):
            o2 = line.ahead(first + k)
            self.far[h, o2] = self.pair(h, o2, partial).astype(BF16)
            self.far_copy(h, o2, line.o).start()

        each(last - first, one)
        if last == line.outer - 1:
            self.total[h] = self.pair(h, line.o, partial)

    def end(self, h):
        line = self.line

        def one(k):
            source = line.behind(k)
            self.far_copy(h, line.ahead(0), source).wait_recv()
            self.total[h] += self.far_in[h, source].astype(F32)

        each(line.outer - 1, one)
        return self.total[h]

    def drain(self, h):
        line = self.line
        if line.inner == 2:
            each(line.outer, lambda k: [copy.wait_send() for copy in self.near_copies(h, k)])
        each(line.outer - 1, lambda k: self.far_copy(h, line.ahead(k), line.o).wait_send())


def kernel(
    rows_n, cols_n, scale,
    coords, features_in, weight, cotangent_in, values,
    activated_out, dfeatures_out, dweight_out,
    features, cotangent, activated, dfeatures, dweight, moved,
    xg, xg_sent, xg_landed,
    dense, flipped,
    c_near, c_near_in, c_far, c_far_in, c_total, c_ns, c_nl, c_fs, c_fl,
    sg, sg_sent, sg_landed,
    grad,
    e_near, e_near_in, e_far, e_far_in, e_total, e_ns, e_nl, e_fs, e_fl,
    w1, w1_in, w1_sent, w1_landed,
    w2, w2_in, w2_sent, w2_landed,
    wcopy, wide, mixed, stock, turned, fetched, kept,
):
    r, c = lax.axis_index("row"), lax.axis_index("col")
    row = Line("row", rows_n, lambda index: (index, c))
    col = Line("col", cols_n, lambda index: (r, index))
    own, hidden = features.shape
    width = hidden // PARTS
    slots, block = values.shape[0], values.shape[1]

    barrier = pltpu.get_barrier_semaphore()
    each(rows_n - 1, lambda k: pl.semaphore_signal(
        barrier, inc=1, device_id=row.device(lax.rem(r + k + 1, rows_n)), device_id_type=MESH))
    each(cols_n - 1, lambda k: pl.semaphore_signal(
        barrier, inc=1, device_id=col.device(lax.rem(c + k + 1, cols_n)), device_id_type=MESH))
    fetch_values = pltpu.make_async_copy(values, stock.at[pl.ds(0, slots)], fetched.at[0])
    fetch_weight = pltpu.make_async_copy(weight, wide, fetched.at[1])
    fetch_features = pltpu.make_async_copy(features_in, features, moved.at[0])
    fetch_cotangent = pltpu.make_async_copy(cotangent_in, cotangent, moved.at[1])
    fetch_features.start()
    fetch_values.start()
    fetch_cotangent.start()
    fetch_weight.start()
    fetch_features.wait()
    for h in range(PARTS):
        xg[h, r] = features[:, h * width:(h + 1) * width].astype(BF16)
    stock[slots] = jnp.zeros((block, block), BF16)
    pl.semaphore_wait(barrier, rows_n + cols_n - 2)

    xs = Gather(row, xg, xg_sent, xg_landed)
    for h in range(PARTS):
        xs.start(h)

    row_blocks, col_blocks = cols_n * own // block, rows_n * own // block
    per = own // block
    short = slots <= 16
    keys = [coords[0, s] * col_blocks + coords[1, s] for s in range(slots)] if short else None

    def place(i):
        for j in range(col_blocks):
            def look(s, found):
                key = keys[s] if short else coords[0, s] * col_blocks + coords[1, s]
                return jnp.where(key == i * col_blocks + j, s, found)

            found = jnp.int32(slots)
            if short:
                for s in range(slots):
                    found = look(s, found)
            else:
                found = lax.fori_loop(0, slots, look, found)
            if per == 1:
                rows, lead = pl.ds(0, block), i
            else:
                rows, lead = pl.ds((i % per) * block, block), i // per
            dense[lead, rows, j * block:(j + 1) * block] = stock[found]
            flipped[lead, j * block:(j + 1) * block, rows] = turned[found]

    def turn(s):
        turned[s] = stock[s].T

    fetch_values.wait()
    each(slots + 1, turn)
    half = row_blocks // 2
    each(half, place)
    each(row.outer - 1, lambda k: xs.relay(0, k))
    each(row_blocks - half, lambda k: place(half + k))
    for h in range(1, PARTS):
        each(row.outer - 1, lambda k: xs.relay(h, k))

    agg = Scatter(col, c_near, c_near_in, c_far, c_far_in, c_total, (c_ns, c_nl, c_fs, c_fl),
                  (PARTS,) + (1,) * (PARTS - 1))

    tall = own // PARTS

    def forward(p, side, parts):
        rows = jnp.concatenate(
            [dense[o2 * col.inner + side, p * tall:(p + 1) * tall, :] for o2 in range(col.outer)], axis=0)
        full = jnp.concatenate([xg[h].reshape(rows_n * own, width) for h in parts], axis=1)
        return dot(rows, full).reshape(col.outer, tall, full.shape[1])

    def kept_block(p, index):
        return kept[p, index // col.inner]

    for h in range(PARTS):
        if row.inner == 2:
            each(row.outer, lambda k: xs.passed(h, k))
        if col.inner == 2:
            c_near[0, :, :, h * width:(h + 1) * width] = forward(0, 1 - col.i, (h,)).astype(BF16)
            agg.start(0, None, h)
    for p in range(1, PARTS):
        if col.inner == 2:
            c_near[p] = forward(p, 1 - col.i, range(PARTS)).astype(BF16)
            agg.start(p, None)
    for p in range(PARTS):
        kept[p] = forward(p, col.i, range(PARTS))
    fetch_weight.wait()
    fetch_cotangent.wait()
    wcopy[...] = wide[...].astype(BF16)

    slopes = Chain(col, sg, sg_sent, sg_landed)

    def own_slope(p):
        span = slice(p * tall, (p + 1) * tall)
        part = agg.end(p).astype(BF16)
        total = dot(part, wcopy[...])
        sigma = jax.nn.sigmoid(total)
        slope = cotangent[span, :].astype(F32) * (sigma * (1.0 + total * (1.0 - sigma)))
        sg[p, c] = slope.astype(BF16)
        slopes.start(p)
        mixed[span, :] = part
        activated[span, :] = total * sigma

    hops = col.outer - 1
    for p in range(PARTS):
        early = (hops + 1) // 2 if p else hops
        agg.middle(p, kept_block, 0, early)
        if p:
            own_slope(p - 1)
            agg.middle(p, kept_block, early, hops)
            each(min(hops, 1), lambda k: slopes.relay(k, p - 1, None))
    own_slope(PARTS - 1)
    give_activated = pltpu.make_async_copy(activated, activated_out, moved.at[2])
    give_dfeatures = pltpu.make_async_copy(dfeatures, dfeatures_out, moved.at[3])
    give_dweight = pltpu.make_async_copy(dweight, dweight_out, moved.at[4])
    give_activated.start()

    def both(index):
        return jnp.concatenate([sg[p, index] for p in range(PARTS)], axis=0)

    share = hidden // rows_n
    w1[...] = dot(mixed[...], both(c), 0, 0).reshape(rows_n, share, hidden).astype(BF16)

    def w1_copy(k):
        to = lax.rem(r + k + 1, rows_n)
        return remote(w1.at[to], w1_in.at[r], w1_sent.at[to], w1_landed.at[r], row.device(to))

    each(rows_n - 1, lambda k: w1_copy(k).start())

    def add(index, h):
        pair = [(index // col.inner) * col.inner + i for i in range(col.inner)]
        span = slice(h * width, (h + 1) * width)
        left = jnp.concatenate([flipped[i] for i in pair], axis=1)
        right = jnp.concatenate([sg[p, i, :, span] for i in pair for p in range(PARTS)], axis=0)
        grad[h] += dot(left, right)

    def add_first(index):
        add(index, 0)

    for h in range(PARTS):
        grad[h] = jnp.zeros(grad.shape[1:], F32)
    alone = add_first if col.inner == 1 else None
    for p in range(PARTS):
        seen = min(hops, 1) if p < PARTS - 1 else 0
        each(hops - seen, lambda k: slopes.relay(seen + k, p, alone if p == PARTS - 1 else None))
    if col.inner == 1:
        add_first(c)

    nodes = Scatter(row, e_near, e_near_in, e_far, e_far_in, e_total, (e_ns, e_nl, e_fs, e_fl),
                    (1,) * PARTS)

    def term(h, index):
        return grad[h, pl.ds(pl.multiple_of(index * own, own), own), :]

    def w1_wait(k):
        source = lax.rem(r + rows_n - k - 1, rows_n)
        remote(w1.at[source], w1_in.at[source], w1_sent.at[source], w1_landed.at[source],
               row.device(source)).wait_recv()
        return source

    def w2_copy(k):
        to = lax.rem(c + k + 1, cols_n)
        return remote(w2.at[to], w2_in.at[c], w2_sent.at[to], w2_landed.at[c], col.device(to))

    def w2_wait(k):
        source = lax.rem(c + cols_n - k - 1, cols_n)
        remote(w2.at[source], w2_in.at[source], w2_sent.at[source], w2_landed.at[source],
               col.device(source)).wait_recv()

    each(rows_n - 1, w1_wait)
    w1_in[r] = w1[r]
    weight_sum = jnp.sum(w1_in[...].astype(F32), axis=0)
    w2[...] = weight_sum.T.reshape(cols_n, hidden // cols_n, share).astype(w2.dtype)
    each(cols_n - 1, lambda k: w2_copy(k).start())
    w2_in[c] = w2[c]

    for p in range(PARTS):
        if col.inner == 2:
            use = add_first if p == PARTS - 1 else None
            slopes.passed(-1, p, use)
            each(hops, lambda k: slopes.passed(k, p, use))
    for h in range(PARTS):
        if h:
            each(col.outer, lambda k: add(k * col.inner, h))
        nodes.start(h, term)
    for h in range(PARTS):
        nodes.middle(h, term, 0, row.outer - 1)

    each(cols_n - 1, w2_wait)
    dweight[...] = jnp.sum(w2_in[...].astype(F32), axis=0) * scale
    give_dweight.start()

    out = None
    for h in range(PARTS):
        grad16 = nodes.end(h).astype(BF16)
        piece = dot(grad16, wcopy[:, h * width:(h + 1) * width], 1, 1)
        out = piece if out is None else out + piece
    dfeatures[...] = out
    give_dfeatures.start()

    for h in range(PARTS):
        xs.drain(h)
        agg.drain(h)
        slopes.drain(h)
        nodes.drain(h)
    each(rows_n - 1, lambda k: w1_copy(k).wait_send())
    each(cols_n - 1, lambda k: w2_copy(k).wait_send())
    for give in (give_activated, give_dweight, give_dfeatures):
        give.wait()


def hand_over(a, b, c, a_out, b_out, c_out, a_held, b_held, c_held, sems):
    rows = ((a, a_held, a_out), (b, b_held, b_out), (c, c_held, c_out))
    ins = [pltpu.make_async_copy(src, held, sems.at[0, k]) for k, (src, held, _) in enumerate(rows)]
    outs = [pltpu.make_async_copy(held, dst, sems.at[1, k]) for k, (_, held, dst) in enumerate(rows)]
    for copy in ins:
        copy.start()
    for copy, after in zip(ins, outs):
        copy.wait()
        after.start()
    for copy in outs:
        copy.wait()


def on_device(rows_n, cols_n, features, weight, cotangent, block_values, block_coords):
    values, coords = block_values[0, 0], block_coords[0, 0]
    own, hidden = features.shape
    width = hidden // PARTS
    row_in, col_in = inner_size(rows_n), inner_size(cols_n)
    row_out, col_out = rows_n // row_in, cols_n // col_in
    scale = 1.0 / (own * rows_n * cols_n) ** 0.5
    share_r, share_c = hidden // rows_n, hidden // cols_n
    dma = pltpu.SemaphoreType.DMA

    def gather_scratch(count, outer):
        return [
            pltpu.VMEM((PARTS, count, own, width), BF16),
            dma((PARTS, 2 * outer)),
            dma((PARTS, count)),
        ]

    def scatter_scratch(outer, piece):
        return (
            [pltpu.VMEM((PARTS, outer) + piece, BF16)] * 4
            + [pltpu.VMEM((PARTS,) + piece, F32)]
            + [dma((PARTS, PARTS, outer))] * 2
            + [dma((PARTS, outer))] * 2
        )

    scratch = (
        [
            pltpu.VMEM((own, hidden), F32),
            pltpu.VMEM((own, hidden), BF16),
            pltpu.VMEM((own, hidden), F32),
            pltpu.VMEM((own, hidden), F32),
            pltpu.VMEM((share_c, share_r), F32),
            dma((5,)),
        ]
        + gather_scratch(rows_n, row_out)
        + [
            pltpu.VMEM((cols_n, own, rows_n * own), BF16),
            pltpu.VMEM((cols_n, rows_n * own, own), BF16),
        ]
        + scatter_scratch(col_out, (own // PARTS, hidden))
        + [
            pltpu.VMEM((PARTS, cols_n, own // PARTS, hidden), BF16),
            dma((PARTS, col_out, 3)),
            dma((PARTS, cols_n)),
        ]
        + [pltpu.VMEM((PARTS, rows_n * own, width), F32)]
        + scatter_scratch(row_out, (own, width))
        + [pltpu.VMEM((rows_n, share_r, hidden), BF16)] * 2
        + [dma((rows_n,))] * 2
        + [pltpu.VMEM((cols_n, share_c, share_r), BF16)] * 2
        + [dma((cols_n,))] * 2
        + [
            pltpu.VMEM((hidden, hidden), BF16),
            pltpu.VMEM((hidden, hidden), F32),
            pltpu.VMEM((own, hidden), BF16),
            pltpu.VMEM((values.shape[0] + 1,) + values.shape[1:], BF16),
            pltpu.VMEM((values.shape[0] + 1,) + values.shape[1:], BF16),
            dma((2,)),
            pltpu.VMEM((PARTS, col_out, own // PARTS, hidden), F32),
        ]
    )
    anywhere = pl.BlockSpec(memory_space=pl.ANY)
    results = pl.pallas_call(
        functools.partial(kernel, rows_n, cols_n, scale),
        out_shape=(
            jax.ShapeDtypeStruct((own, hidden), F32),
            jax.ShapeDtypeStruct((own, hidden), F32),
            jax.ShapeDtypeStruct((share_c, share_r), F32),
        ),
        in_specs=[pl.BlockSpec(memory_space=pltpu.SMEM)] + [anywhere] * 4,
        out_specs=(anywhere,) * 3,
        scratch_shapes=scratch,
        compiler_params=pltpu.CompilerParams(
            collective_id=0, has_side_effects=True, vmem_limit_bytes=56 * 1024 * 1024
        ),
    )(coords, features, weight, cotangent, values)
    ours, theirs, flat = pl.pallas_call(
        hand_over,
        out_shape=tuple(jax.ShapeDtypeStruct(a.shape, a.dtype) for a in results),
        in_specs=[pl.BlockSpec(memory_space=pltpu.HBM)] * 3,
        out_specs=(pl.BlockSpec(memory_space=pltpu.HBM),) * 3,
        scratch_shapes=[pltpu.VMEM(a.shape, a.dtype) for a in results] + [dma((2, 3))],
        compiler_params=pltpu.CompilerParams(vmem_limit_bytes=60 * 1024 * 1024),
    )(*results)
    return ours, theirs, flat.T


def solution(mesh):
    placed = (
        P(("col", "row"), None),
        P(),
        P(("row", "col"), None),
        P("row", "col", None, None, None),
        P("row", "col", None, None),
    )
    return jax.shard_map(
        functools.partial(on_device, mesh.shape["row"], mesh.shape["col"]),
        mesh=mesh,
        in_specs=placed,
        out_specs=(P(("row", "col"), None), P(("col", "row"), None), P("row", "col")),
        check_vma=False,
    )
```

```python
import functools

import jax
import jax.numpy as jnp
from jax import lax
from jax.experimental import pallas as pl
from jax.experimental.pallas import tpu as pltpu
from jax.sharding import PartitionSpec as P

MESH = pl.DeviceIdType.MESH
PARTS = 2
F32, BF16 = jnp.float32, jnp.bfloat16


def each(count, body):
    if count <= 8:
        for k in range(count):
            body(k)
    else:
        lax.fori_loop(0, count, lambda k, carry: (body(k), carry)[1], 0)


def inner_size(count):
    return 2 if count % 2 == 0 else 1


def dot(a, b, left=1, right=0):
    return lax.dot_general(a, b, (((left,), (right,)), ((), ())), preferred_element_type=F32)


def remote(src, dst, sent, landed, device):
    return pltpu.make_async_remote_copy(
        src_ref=src, dst_ref=dst, send_sem=sent, recv_sem=landed, device_id=device, device_id_type=MESH
    )


class Line:
    def __init__(self, name, count, device):
        self.count, self.device = count, device
        self.inner = inner_size(count)
        self.outer = count // self.inner
        self.me = lax.axis_index(name)
        self.o = self.me // self.inner
        self.i = self.me % self.inner

    def ahead(self, k):
        return lax.rem(self.o + k + 1, self.outer)

    def behind(self, k):
        return lax.rem(self.o + self.outer - k - 1, self.outer)

    def offset(self, k):
        if self.outer == 1:
            return 0
        hops = (k + self.outer // 2 - 1) % (self.outer - 1) + 1
        if isinstance(k, int):
            return hops if k < self.outer - 1 else 0
        return jnp.where(k < self.outer - 1, hops, 0)

    def ahead_far(self, k):
        return lax.rem(self.o + self.offset(k), self.outer)

    def behind_far(self, k):
        return lax.rem(self.o + self.outer - self.offset(k), self.outer)

    def mate(self):
        return self.device(self.o * self.inner + 1 - self.i)


class Gather:
    def __init__(self, line, buf, sent, landed):
        self.line, self.buf, self.sent, self.landed = line, buf, sent, landed

    def copy(self, h, index, slot, device):
        piece = self.buf.at[h, index]
        return remote(piece, piece, self.sent.at[h, slot], self.landed.at[h, index], device)

    def start(self, h):
        line = self.line

        def far(k):
            self.copy(h, line.me, k, line.device(line.ahead(k) * line.inner + line.i)).start()

        if line.inner == 2:
            self.copy(h, line.me, line.outer - 1, line.mate()).start()
        each(line.outer - 1, far)

    def any_peer(self):
        line = self.line
        return line.device(lax.rem(line.me + 1, line.count))

    def relay(self, h, k):
        line = self.line
        index = line.behind(k) * line.inner + line.i
        self.copy(h, index, k, self.any_peer()).wait_recv()
        if line.inner == 2:
            self.copy(h, index, line.outer + k, line.mate()).start()
        return index

    def passed(self, h, k):
        line = self.line
        index = line.behind(k - 1) * line.inner + 1 - line.i
        self.copy(h, index, 0, self.any_peer()).wait_recv()
        return index

    def drain(self, h):
        line = self.line
        slots = 2 * line.outer - 1 if line.inner == 2 else line.outer - 1
        each(slots, lambda k: self.copy(h, line.me, k, self.any_peer()).wait_send())


class Chain:
    def __init__(self, line, buf, sent, landed):
        self.line, self.buf, self.sent, self.landed = line, buf, sent, landed

    def copy(self, h, index, way, device):
        piece = self.buf.at[h, index]
        return remote(
            piece, piece, self.sent.at[h, index // self.line.inner, way], self.landed.at[h, index], device
        )

    def side(self, way):
        line = self.line
        step = 1 if way == 0 else -1
        there = line.o + step
        inside = there < line.outer if way == 0 else there >= 0
        device = line.device(lax.rem(there + line.outer, line.outer) * line.inner + line.i)
        return inside, device

    def spread(self, h, index, ways):
        for way in ways:
            inside, device = self.side(way)

            @pl.when(inside)
            def _():
                self.copy(h, index, way, device).start()

        if self.line.inner == 2:
            self.copy(h, index, 2, self.line.mate()).start()

    def start(self, h):
        self.spread(h, self.line.me, (0, 1))

    def other(self):
        line = self.line
        return line.device(lax.rem(line.me + 1, line.count))

    def each_source(self, k, body):
        line = self.line
        for way, source in ((0, line.o - 1 - k), (1, line.o + 1 + k)):
            pl.when(jnp.logical_and(source >= 0, source < line.outer))(
                functools.partial(body, way, source))

    def relay(self, k, h, use):
        def arrived(way, source):
            index = source * self.line.inner + self.line.i
            self.copy(h, index, way, self.other()).wait_recv()
            self.spread(h, index, (way,))
            if use is not None:
                use(index)

        self.each_source(k, arrived)

    def passed(self, k, h, use):
        def arrived(way, source):
            index = source * self.line.inner + 1 - self.line.i
            self.copy(h, index, 2, self.other()).wait_recv()
            if use is not None:
                use(index)

        if isinstance(k, int) and k < 0:
            arrived(2, self.line.o)
        else:
            self.each_source(k, arrived)

    def drain(self, h):
        line = self.line

        def one(source):
            index = source * line.inner + line.i
            for way in (0, 1):
                inside, device = self.side(way)
                went = source <= line.o if way == 0 else source >= line.o

                @pl.when(jnp.logical_and(inside, went))
                def _():
                    self.copy(h, index, way, device).wait_send()

            if line.inner == 2:
                self.copy(h, index, 2, line.mate()).wait_send()

        each(line.outer, one)


class Scatter:
    def __init__(self, line, near, near_in, far, far_in, total, sems):
        self.line, self.total = line, total
        self.near, self.near_in, self.far, self.far_in = near, near_in, far, far_in
        self.near_sent, self.near_landed, self.far_sent, self.far_landed = sems

    def near_copy(self, h, o2):
        return remote(
            self.near.at[h, o2], self.near_in.at[h, o2], self.near_sent.at[h, o2],
            self.near_landed.at[h, o2], self.line.mate(),
        )

    def far_copy(self, h, o2, source):
        return remote(
            self.far.at[h, o2], self.far_in.at[h, source], self.far_sent.at[h, o2],
            self.far_landed.at[h, source], self.line.device(o2 * self.line.inner + self.line.i),
        )

    def start(self, h, partial):
        line = self.line

        def one(k):
            o2 = line.ahead_far(k)
            if partial is not None:
                self.near[h, o2] = partial(h, o2 * line.inner + 1 - line.i).astype(BF16)
            self.near_copy(h, o2).start()

        if line.inner == 2:
            each(line.outer, one)

    def pair(self, h, o2, partial):
        line = self.line
        value = partial(h, o2 * line.inner + line.i)
        if line.inner == 2:
            self.near_copy(h, o2).wait_recv()
            value = value + self.near_in[h, o2].astype(F32)
        return value

    def middle(self, h, partial, first, last):
        line = self.line

        def one(k):
            o2 = line.ahead_far(first + k)
            self.far[h, o2] = self.pair(h, o2, partial).astype(BF16)
            self.far_copy(h, o2, line.o).start()

        each(last - first, one)
        if last == line.outer - 1:
            self.total[h] = self.pair(h, line.o, partial)

    def end(self, h):
        line = self.line

        def one(k):
            source = line.behind_far(k)
            self.far_copy(h, line.ahead_far(0), source).wait_recv()
            self.total[h] += self.far_in[h, source].astype(F32)

        each(line.outer - 1, one)
        return self.total[h]

    def drain(self, h):
        line = self.line
        if line.inner == 2:
            each(line.outer, lambda k: self.near_copy(h, k).wait_send())
        each(line.outer - 1, lambda k: self.far_copy(h, line.ahead_far(k), line.o).wait_send())


def kernel(
    rows_n, cols_n, scale,
    coords, features, weight, cotangent, values,
    activated, dfeatures, dweight,
    xg, xg_sent, xg_landed,
    dense, flipped,
    c_near, c_near_in, c_far, c_far_in, c_total, c_ns, c_nl, c_fs, c_fl,
    sg, sg_sent, sg_landed,
    grad,
    e_near, e_near_in, e_far, e_far_in, e_total, e_ns, e_nl, e_fs, e_fl,
    w1, w1_in, w1_sent, w1_landed,
    w2, w2_in, w2_sent, w2_landed,
    wcopy, wide, mixed, stock, turned, fetched, kept,
):
    r, c = lax.axis_index("row"), lax.axis_index("col")
    row = Line("row", rows_n, lambda index: (index, c))
    col = Line("col", cols_n, lambda index: (r, index))
    own, hidden = features.shape
    width = hidden // PARTS
    slots, block = values.shape[0], values.shape[1]

    barrier = pltpu.get_barrier_semaphore()
    each(rows_n - 1, lambda k: pl.semaphore_signal(
        barrier, inc=1, device_id=row.device(lax.rem(r + k + 1, rows_n)), device_id_type=MESH))
    each(cols_n - 1, lambda k: pl.semaphore_signal(
        barrier, inc=1, device_id=col.device(lax.rem(c + k + 1, cols_n)), device_id_type=MESH))
    fetch_values = pltpu.make_async_copy(values, stock.at[pl.ds(0, slots)], fetched.at[0])
    fetch_weight = pltpu.make_async_copy(weight, wide, fetched.at[1])
    fetch_values.start()
    fetch_weight.start()
    for h in range(PARTS):
        xg[h, r] = features[:, h * width:(h + 1) * width].astype(BF16)
    stock[slots] = jnp.zeros((block, block), BF16)
    pl.semaphore_wait(barrier, rows_n + cols_n - 2)

    xs = Gather(row, xg, xg_sent, xg_landed)
    for h in range(PARTS):
        xs.start(h)

    row_blocks, col_blocks = cols_n * own // block, rows_n * own // block
    per = own // block
    short = slots <= 16
    keys = [coords[0, s] * col_blocks + coords[1, s] for s in range(slots)] if short else None

    def place(i):
        for j in range(col_blocks):
            def look(s, found):
                key = keys[s] if short else coords[0, s] * col_blocks + coords[1, s]
                return jnp.where(key == i * col_blocks + j, s, found)

            found = jnp.int32(slots)
            if short:
                for s in range(slots):
                    found = look(s, found)
            else:
                found = lax.fori_loop(0, slots, look, found)
            if per == 1:
                rows, lead = pl.ds(0, block), i
            else:
                rows, lead = pl.ds((i % per) * block, block), i // per
            dense[lead, rows, j * block:(j + 1) * block] = stock[found]
            flipped[lead, j * block:(j + 1) * block, rows] = turned[found]

    def turn(s):
        turned[s] = stock[s].T

    fetch_values.wait()
    each(slots + 1, turn)
    half = row_blocks // 2
    each(half, place)
    each(row.outer - 1, lambda k: xs.relay(0, k))
    each(row_blocks - half, lambda k: place(half + k))
    for h in range(1, PARTS):
        each(row.outer - 1, lambda k: xs.relay(h, k))

    agg = Scatter(col, c_near, c_near_in, c_far, c_far_in, c_total, (c_ns, c_nl, c_fs, c_fl))

    tall = own // PARTS

    def forward(p, side):
        rows = jnp.concatenate(
            [dense[o2 * col.inner + side, p * tall:(p + 1) * tall, :] for o2 in range(col.outer)], axis=0)
        full = jnp.concatenate([xg[h].reshape(rows_n * own, width) for h in range(PARTS)], axis=1)
        return dot(rows, full).reshape(col.outer, tall, hidden)

    def kept_block(p, index):
        return kept[p, index // col.inner]

    for h in range(PARTS):
        if row.inner == 2:
            each(row.outer, lambda k: xs.passed(h, k))
    for p in range(PARTS):
        if col.inner == 2:
            c_near[p] = forward(p, 1 - col.i).astype(BF16)
        agg.start(p, None)
    for p in range(PARTS):
        kept[p] = forward(p, col.i)
    fetch_weight.wait()
    wcopy[...] = wide[...].astype(BF16)

    slopes = Chain(col, sg, sg_sent, sg_landed)

    def own_slope(p):
        span = slice(p * tall, (p + 1) * tall)
        part = agg.end(p).astype(BF16)
        total = dot(part, wcopy[...])
        sigma = jax.nn.sigmoid(total)
        slope = cotangent[span, :].astype(F32) * (sigma * (1.0 + total * (1.0 - sigma)))
        sg[p, c] = slope.astype(BF16)
        slopes.start(p)
        mixed[span, :] = part
        activated[span, :] = total * sigma

    hops = col.outer - 1
    for p in range(PARTS):
        early = (hops + 1) // 2 if p else hops
        agg.middle(p, kept_block, 0, early)
        if p:
            own_slope(p - 1)
            agg.middle(p, kept_block, early, hops)
            each(min(hops, 1), lambda k: slopes.relay(k, p - 1, None))
    own_slope(PARTS - 1)

    def both(index):
        return jnp.concatenate([sg[p, index] for p in range(PARTS)], axis=0)

    share = hidden // rows_n
    w1[...] = dot(mixed[...], both(c), 0, 0).reshape(rows_n, share, hidden).astype(BF16)

    def w1_copy(k):
        to = lax.rem(r + k + 1, rows_n)
        return remote(w1.at[to], w1_in.at[r], w1_sent.at[to], w1_landed.at[r], row.device(to))

    each(rows_n - 1, lambda k: w1_copy(k).start())

    def add(index, h):
        pair = [(index // col.inner) * col.inner + i for i in range(col.inner)]
        span = slice(h * width, (h + 1) * width)
        left = jnp.concatenate([flipped[i] for i in pair], axis=1)
        right = jnp.concatenate([sg[p, i, :, span] for i in pair for p in range(PARTS)], axis=0)
        grad[h] += dot(left, right)

    def add_all(index):
        for h in range(PARTS):
            add(index, h)

    for h in range(PARTS):
        grad[h] = jnp.zeros(grad.shape[1:], F32)
    alone = add_all if col.inner == 1 else None
    for p in range(PARTS):
        seen = min(hops, 1) if p < PARTS - 1 else 0
        each(hops - seen, lambda k: slopes.relay(seen + k, p, alone if p == PARTS - 1 else None))
    if col.inner == 1:
        add_all(c)

    nodes = Scatter(row, e_near, e_near_in, e_far, e_far_in, e_total, (e_ns, e_nl, e_fs, e_fl))

    def term(h, index):
        return grad[h, pl.ds(pl.multiple_of(index * own, own), own), :]

    def w1_wait(k):
        source = lax.rem(r + rows_n - k - 1, rows_n)
        remote(w1.at[source], w1_in.at[source], w1_sent.at[source], w1_landed.at[source],
               row.device(source)).wait_recv()
        return source

    def w2_copy(k):
        to = lax.rem(c + k + 1, cols_n)
        return remote(w2.at[to], w2_in.at[c], w2_sent.at[to], w2_landed.at[c], col.device(to))

    def w2_wait(k):
        source = lax.rem(c + cols_n - k - 1, cols_n)
        remote(w2.at[source], w2_in.at[source], w2_sent.at[source], w2_landed.at[source],
               col.device(source)).wait_recv()

    each(rows_n - 1, w1_wait)
    w1_in[r] = w1[r]
    weight_sum = jnp.sum(w1_in[...].astype(F32), axis=0)
    w2[...] = weight_sum.T.reshape(cols_n, hidden // cols_n, share).astype(w2.dtype)
    each(cols_n - 1, lambda k: w2_copy(k).start())
    w2_in[c] = w2[c]

    for p in range(PARTS):
        if col.inner == 2:
            use = add_all if p == PARTS - 1 else None
            slopes.passed(-1, p, use)
            each(hops, lambda k: slopes.passed(k, p, use))
    for h in range(PARTS):
        nodes.start(h, term)
    for h in range(PARTS):
        nodes.middle(h, term, 0, row.outer - 1)

    out = None
    for h in range(PARTS):
        grad16 = nodes.end(h).astype(BF16)
        piece = dot(grad16, wcopy[:, h * width:(h + 1) * width], 1, 1)
        out = piece if out is None else out + piece
    dfeatures[...] = out

    each(cols_n - 1, w2_wait)
    dweight[...] = jnp.sum(w2_in[...].astype(F32), axis=0) * scale

    for h in range(PARTS):
        xs.drain(h)
        agg.drain(h)
        slopes.drain(h)
        nodes.drain(h)
    each(rows_n - 1, lambda k: w1_copy(k).wait_send())
    each(cols_n - 1, lambda k: w2_copy(k).wait_send())


def hand_over(a, b, c, a_out, b_out, c_out, a_held, b_held, c_held, sems):
    rows = ((a, a_held, a_out), (b, b_held, b_out), (c, c_held, c_out))
    ins = [pltpu.make_async_copy(src, held, sems.at[0, k]) for k, (src, held, _) in enumerate(rows)]
    outs = [pltpu.make_async_copy(held, dst, sems.at[1, k]) for k, (_, held, dst) in enumerate(rows)]
    for copy in ins:
        copy.start()
    for copy, after in zip(ins, outs):
        copy.wait()
        after.start()
    for copy in outs:
        copy.wait()


def on_device(rows_n, cols_n, features, weight, cotangent, block_values, block_coords):
    values, coords = block_values[0, 0], block_coords[0, 0]
    own, hidden = features.shape
    width = hidden // PARTS
    row_in, col_in = inner_size(rows_n), inner_size(cols_n)
    row_out, col_out = rows_n // row_in, cols_n // col_in
    scale = 1.0 / (own * rows_n * cols_n) ** 0.5
    share_r, share_c = hidden // rows_n, hidden // cols_n
    dma = pltpu.SemaphoreType.DMA

    def gather_scratch(count, outer):
        return [
            pltpu.VMEM((PARTS, count, own, width), BF16),
            dma((PARTS, 2 * outer)),
            dma((PARTS, count)),
        ]

    def scatter_scratch(outer, piece):
        return (
            [pltpu.VMEM((PARTS, outer) + piece, BF16)] * 4
            + [pltpu.VMEM((PARTS,) + piece, F32)]
            + [dma((PARTS, outer))] * 4
        )

    scratch = (
        gather_scratch(rows_n, row_out)
        + [
            pltpu.VMEM((cols_n, own, rows_n * own), BF16),
            pltpu.VMEM((cols_n, rows_n * own, own), BF16),
        ]
        + scatter_scratch(col_out, (own // PARTS, hidden))
        + [
            pltpu.VMEM((PARTS, cols_n, own // PARTS, hidden), BF16),
            dma((PARTS, col_out, 3)),
            dma((PARTS, cols_n)),
        ]
        + [pltpu.VMEM((PARTS, rows_n * own, width), F32)]
        + scatter_scratch(row_out, (own, width))
        + [pltpu.VMEM((rows_n, share_r, hidden), BF16)] * 2
        + [dma((rows_n,))] * 2
        + [pltpu.VMEM((cols_n, share_c, share_r), BF16)] * 2
        + [dma((cols_n,))] * 2
        + [
            pltpu.VMEM((hidden, hidden), BF16),
            pltpu.VMEM((hidden, hidden), F32),
            pltpu.VMEM((own, hidden), BF16),
            pltpu.VMEM((values.shape[0] + 1,) + values.shape[1:], BF16),
            pltpu.VMEM((values.shape[0] + 1,) + values.shape[1:], BF16),
            dma((2,)),
            pltpu.VMEM((PARTS, col_out, own // PARTS, hidden), F32),
        ]
    )
    vmem = pl.BlockSpec(memory_space=pltpu.VMEM)
    anywhere = pl.BlockSpec(memory_space=pl.ANY)
    results = pl.pallas_call(
        functools.partial(kernel, rows_n, cols_n, scale),
        out_shape=(
            jax.ShapeDtypeStruct((own, hidden), F32),
            jax.ShapeDtypeStruct((own, hidden), F32),
            jax.ShapeDtypeStruct((share_c, share_r), F32),
        ),
        in_specs=[pl.BlockSpec(memory_space=pltpu.SMEM), vmem, anywhere, vmem, anywhere],
        out_specs=(vmem, vmem, vmem),
        scratch_shapes=scratch,
        compiler_params=pltpu.CompilerParams(
            collective_id=0, has_side_effects=True, vmem_limit_bytes=56 * 1024 * 1024
        ),
    )(coords, features, weight, cotangent, values)
    ours, theirs, flat = pl.pallas_call(
        hand_over,
        out_shape=tuple(jax.ShapeDtypeStruct(a.shape, a.dtype) for a in results),
        in_specs=[pl.BlockSpec(memory_space=pltpu.HBM)] * 3,
        out_specs=(pl.BlockSpec(memory_space=pltpu.HBM),) * 3,
        scratch_shapes=[pltpu.VMEM(a.shape, a.dtype) for a in results] + [dma((2, 3))],
        compiler_params=pltpu.CompilerParams(vmem_limit_bytes=60 * 1024 * 1024),
    )(*results)
    return ours, theirs, flat.T


def solution(mesh):
    placed = (
        P(("col", "row"), None),
        P(),
        P(("row", "col"), None),
        P("row", "col", None, None, None),
        P("row", "col", None, None),
    )
    return jax.shard_map(
        functools.partial(on_device, mesh.shape["row"], mesh.shape["col"]),
        mesh=mesh,
        in_specs=placed,
        out_specs=(P(("row", "col"), None), P(("col", "row"), None), P("row", "col")),
        check_vma=False,
    )
```
